256 devices in a mesh: dp: 32 (over z, x), sub: 8 (over y, core).
Axes of the slice: x: 4, y: 4, z: 8, core: 2. Of those that a mesh axis runs over, the one named last changes fastest.
Arguments:
- tokens: bfloat16 [131072, 1024], P(('dp', 'sub')), may hold values from -6 to 6
- lengths: int32 [32, 8, 4], P('dp', 'sub'), may hold values from 1 to 341, 512 in all within a row
- w_up: bfloat16 [4096, 1024], P('dp'), may hold values from -0.1875 to 0.1875
- up_bias: bfloat16 [4096], P('dp'), may hold values from -3 to 3
- w_down: bfloat16 [4096, 1024], P('dp'), may hold values from -0.09375 to 0.09375
- down_bias: float32 [1024], replicated, may hold values from -3 to 3
- ln_gain: float32 [1024], replicated, may hold values from 0.5 to 1.5
- ln_bias: float32 [1024], replicated, may hold values from -0.6 to 0.6
- stored: bfloat16 [65536, 1024], P('dp', 'sub'), may hold values from -6 to 6
- stored_codes: int32 [8, 65536], P('sub', 'dp'), may hold values from 0 to 4095
- new_codes: int32 [8, 1024], P('sub'), may hold values from 0 to 4095
- centroids: float32 [8, 4096, 128], P('sub'), may hold values from -6 to 6
Outputs:
- embeds: bfloat16 [1024, 1024], P('dp', 'sub')
- updated: float32 [8, 4096, 128], P('sub')
The draws below stay inside these ranges and needn't reach their ends.
Inputs may be any that keep to these rules, and one draw needn't show every extreme that they name: The 4 lengths of one block sum to 512; in every block the longest is exactly 341.
All inputs are finite; a program needn't handle non-finite values.
Results may differ from the reference program's by a relative error of at most 0.015.
Values may be sent and summed in bfloat16 or wider, within the bound.
A program may use at most 128 MiB of HBM per device.

```python
import math
import jax
import jax.numpy as jnp
import numpy as np
from jax import lax

D = 1024
FF = 4096
SUBS = 8
CODES = 4096
TOK_DEV = 512
PASSAGES_LOCAL = 4
MAX_LEN = 341
SUB_DIM = 128
TOKENS = 131072
PASSAGES = 1024
STORE_ALL = 65536
N_DP = 32
N_SUB = 8


def plant(result, key, low, top_value):
    longest = result.shape.index(max(result.shape))
    spots = []
    for shift in (0, 1):
        where = [jax.random.randint(jax.random.fold_in(key, axis), (), 0, length) for axis, length in enumerate(result.shape)]
        where[longest] = (where[longest] + shift) % result.shape[longest]
        spots.append(tuple(where))
    return result.at[spots[0]].set(low).at[spots[1]].set(top_value)


def levels(key, shape, split, smallest, high):
    def one(position, parts):
        draws = jax.random.uniform(jax.random.fold_in(jax.random.fold_in(key, 6), position), (parts,), jnp.float32, smallest / len(split), high / len(split))
        return jnp.repeat(jnp.exp(draws), shape[position] // parts).reshape((-1,) + (1,) * (len(shape) - position - 1))

    gain = one(*split[0])
    for cut in split[1:]:
        gain = gain * one(*cut)
    return gain


def profile(count, total, reach, skew):
    loads = [(1 << 20) // math.isqrt(grade ** skew) + 1 for grade in range(2, count + 1)]
    surplus, given = total - reach - (count - 1), [1] * (count - 1)
    while surplus > 0:
        free = [i for i in range(count - 1) if given[i] < reach]
        pool, remaining = sum([loads[i] for i in free]), surplus
        for i in free:
            extra = min(reach - given[i], max(1, remaining * loads[i] // pool), surplus)
            given[i] = given[i] + extra
            surplus = surplus - extra
    return np.array([reach] + given)


def uneven_parts(stream_key, amount, total, reach, slope):
    if amount == 2:
        one = jax.random.randint(stream_key, (), max(1, total - reach), min(reach, total - 1) + 1)
        return jnp.stack([one, total - one])
    sizes = jnp.asarray(profile(amount, total, reach, slope), jnp.int32)
    twos = (amount - 1) // 2
    source_of, sink = sizes[1:1 + 2 * twos:2], sizes[2:2 + 2 * twos:2]
    room = jnp.minimum(source_of - 1, reach - sink)
    moved = jax.random.randint(jax.random.fold_in(stream_key, 1), (twos,), 0, 1 << 20) % (room + 1)
    sizes = sizes.at[1:1 + 2 * twos:2].set(source_of - moved).at[2:2 + 2 * twos:2].set(sink + moved)
    return sizes[jax.random.permutation(jax.random.fold_in(stream_key, 2), amount)]


def normal_values(key, dims, width, reach, split=(), held_as=jnp.bfloat16):
    factor_of = levels(key, dims, split, -0.22, 0.18) if split else 1.0
    result = jax.random.normal(key, dims, jnp.float32) * width * factor_of
    return jnp.minimum(jnp.maximum(result, -reach), reach).astype(held_as)


def setup_inputs(seed: int = 0) -> dict:
    key_of = jax.random.split(jax.random.key(seed), 13)
    return {
        "tokens": normal_values(key_of[0], (TOKENS, D), 1.0, 6.0, ((0, 256),)),
        "lengths": jax.vmap(lambda own: uneven_parts(own, PASSAGES_LOCAL, TOK_DEV, MAX_LEN, 2))(jax.random.split(key_of[1], N_DP * N_SUB)).reshape((N_DP, N_SUB, PASSAGES_LOCAL)).astype(jnp.int32),
        "w_up": normal_values(key_of[2], (FF, D), D ** -0.5, 0.1875, ((0, 32),)),
        "up_bias": normal_values(key_of[3], (FF,), 0.5, 3.0, ((0, 32),)),
        "w_down": normal_values(key_of[4], (FF, D), FF ** -0.5, 0.09375, ((0, 32),)),
        "down_bias": normal_values(key_of[5], (D,), 0.5, 3.0, (), jnp.float32),
        "ln_gain": jnp.clip(1.0 + 0.1 * jax.random.normal(key_of[6], (D,), jnp.float32), 0.5, 1.5),
        "ln_bias": normal_values(key_of[7], (D,), 0.1, 0.6, (), jnp.float32),
        "stored": normal_values(key_of[8], (STORE_ALL, D), 1.0, 6.0, ((0, 32), (1, 8))),
        "stored_codes": plant(jax.random.randint(key_of[9], (SUBS, STORE_ALL), 0, CODES), jax.random.fold_in(key_of[9], 1), 0, CODES - 1).astype(jnp.int32),
        "new_codes": plant(jax.random.randint(key_of[10], (SUBS, PASSAGES), 0, CODES), jax.random.fold_in(key_of[10], 1), 0, CODES - 1).astype(jnp.int32),
        "centroids": normal_values(key_of[11], (SUBS, CODES, SUB_DIM), 1.0, 6.0, ((0, 8),), jnp.float32),
    }


def encode_block(tokens, lengths, w_up, up_bias, w_down, down_bias, ln_gain, ln_bias):
    preact = lax.dot_general(tokens, w_up, (((1,), (1,)), ((), ())), preferred_element_type=jnp.float32)
    preact = preact + up_bias.astype(jnp.float32)
    hidden = jax.nn.gelu(preact, approximate=False).astype(jnp.bfloat16)
    ffn = jnp.dot(hidden, w_down, preferred_element_type=jnp.float32) + down_bias
    resid = tokens.astype(jnp.float32) + ffn
    center = resid - lax.optimization_barrier(jnp.mean(resid, axis=-1, keepdims=True))
    spread = lax.optimization_barrier(jnp.mean(center * center, axis=-1, keepdims=True))
    layer_out = (center * lax.rsqrt(spread + 1e-12) * ln_gain + ln_bias).astype(jnp.bfloat16)
    ending = jnp.cumsum(lengths, dtype=jnp.int32)
    opening = ending - lengths
    places = jnp.arange(tokens.shape[0], dtype=jnp.int32)
    member = ((places[None, :] >= opening[:, None]) & (places[None, :] < ending[:, None])).astype(jnp.bfloat16)
    pooled = jnp.dot(member, layer_out, preferred_element_type=jnp.float32) / lengths[:, None].astype(jnp.float32)
    scaling = lax.rsqrt(lax.optimization_barrier(jnp.mean(pooled * pooled, axis=-1, keepdims=True)) + 1e-06)
    return (pooled * scaling).astype(jnp.bfloat16)

def reference(tokens, lengths, w_up, up_bias, w_down, down_bias, ln_gain, ln_bias, stored, stored_codes, new_codes, centroids):
    blocks = tokens.reshape(N_DP * N_SUB, TOK_DEV, D)
    block_lengths = lengths.reshape(N_DP * N_SUB, PASSAGES_LOCAL)

    def encode_one(pair):
        return encode_block(pair[0], pair[1], w_up, up_bias, w_down, down_bias, ln_gain, ln_bias)
    embeds = lax.map(encode_one, (blocks, block_lengths)).reshape(PASSAGES, D)
    vectors = jnp.concatenate([stored, embeds], axis=0)
    codes = jnp.concatenate([stored_codes, new_codes], axis=1)
    row_count = vectors.shape[0]
    by_space = jnp.transpose(vectors.reshape(row_count, SUBS, SUB_DIM), (1, 0, 2))

    def update_one(triple):
        subspace_row_slices, space_codes, old_codes = triple
        centroid_totals = jax.ops.segment_sum(subspace_row_slices.astype(jnp.float32), space_codes, num_segments=CODES)
        counts = jax.ops.segment_sum(jnp.ones(space_codes.shape, jnp.float32), space_codes, num_segments=CODES)
        return (centroid_totals + old_codes) / (counts[:, None] + 1.0)
    updated = lax.map(update_one, (by_space, codes, centroids))
    return (embeds, updated)
```

```python
import functools

import jax
import jax.numpy as jnp
from jax import lax
from jax.experimental import pallas as pl
from jax.experimental.pallas import tpu as pltpu
from jax.sharding import PartitionSpec as P

MESH = pl.DeviceIdType.MESH
NX, NZ, NS = 4, 8, 8
BF, F32 = jnp.bfloat16, jnp.float32

GELU_P = (
    0.7978849411010742,
    0.03633308410644531,
    -3.259497316321358e-05,
    -5.530619455385022e-05,
    3.964744792028796e-06,
    -1.322633664813111e-07,
    1.7561715415226331e-09,
)
GELU_CAP = 30.0

SLOT_UP = (0, 1, 3, 5, 7)
SLOT_DOWN = (0, 2, 4, 6, 7)


def gelu(p):
    t = jnp.minimum(p * p, GELU_CAP)
    q = jnp.full_like(t, GELU_P[-1])
    for coefficient in GELU_P[-2::-1]:
        q = q * t + coefficient
    half = 0.5 * p
    return half + half * jnp.tanh(p * q)


def tidy_block(total):
    n = total.shape[0]
    count = 256.0 * total[:, 128:129, :] + total[:, 129:130, :]
    return jnp.concatenate([total[:, :128, :], count_rows(count, n)], axis=1).astype(BF)


def count_rows(count, n):
    high = jnp.floor(count * (1.0 / 256.0))
    low = count - 256.0 * high
    row = lax.broadcasted_iota(jnp.int32, (n, 16, 128), 1)
    return jnp.where(row == 0, high, jnp.where(row == 1, low, 0.0))


def layer_kernel(
    tokens, w_up, w_down, stored, lengths, up_bias, down_bias, ln_gain, ln_bias, codes,
    e_out, f_out,
    x_buf, gu, gd, acc, ps, pr, sv, tt, ra, rb, rc, ff, bb, em, er, ee, pooled,
    send_sem, recv_sem, local_sem,
):
    dp, s = lax.axis_index("dp"), lax.axis_index("sub")
    z, x, core = dp // NX, dp % NX, s % 2
    quarter = ((s // 2) % 2) * 2 + core

    def z_peer(k):
        return (((z + k + NZ) % NZ) * NX + x, s)

    def x_peer(k):
        return (z * NX + (x + k + NX) % NX, s)

    def s_peer(k):
        return (dp, (s + k) % NS)

    mate = (dp, s + 1 - 2 * core)
    partner = (dp, (s + 2 * core - 1 + NS) % NS)

    used = [0, 0]
    started = []

    def remote(src, dst, device):
        i = used[0]
        used[0] += 1
        copy = pltpu.make_async_remote_copy(
            src_ref=src, dst_ref=dst, send_sem=send_sem.at[i], recv_sem=recv_sem.at[i],
            device_id=device, device_id_type=MESH,
        )
        started.append(copy)
        return copy

    def local(src, dst):
        i = used[1]
        used[1] += 1
        copy = pltpu.make_async_copy(src, dst, local_sem.at[i])
        copy.start()
        return copy

    row0 = pl.multiple_of(quarter * 32, 32)
    load_up = local(w_up.at[pl.ds(row0, 32)], gu.at[0, 0, 0])
    load_down = local(w_down.at[pl.ds(row0, 32)], gd.at[0, 0, 0])
    load_x = local(tokens, x_buf.at[0])
    load_s = local(stored, sv.at[:, pl.ds(0, 128)])

    barrier = pltpu.get_barrier_semaphore()
    peers = [z_peer(k) for k in range(1, NZ)] + [x_peer(k) for k in range(1, NX)] + [s_peer(k) for k in range(1, NS)]
    for device in peers:
        pl.semaphore_signal(barrier, inc=1, device_id=device, device_id_type=MESH)

    lane = lax.broadcasted_iota(jnp.int32, (8, 128), 1)
    own_bias = jnp.where(lane // 32 == quarter, jnp.broadcast_to(up_bias[...].astype(F32), (8, 128)), 0.0)
    own_bias = own_bias + pltpu.roll(own_bias, 64, 1)
    bb[0, 0] = own_bias + pltpu.roll(own_bias, 32, 1)
    sv[:, 128:256] = jnp.ones((2048, 128), BF)

    load_up.wait()
    load_down.wait()
    load_x.wait()
    pl.semaphore_wait(barrier, len(peers))

    flows = {}
    buffers = {"u": gu, "d": gd}

    def piece(kind, jx, slot, half):
        ref = buffers[kind].at[slot // 4, jx, slot % 4]
        return ref if half is None else ref.at[pl.ds(16 * half, 16)]

    def send(kind, axis, direction, src, dst, half):
        device = z_peer(direction) if axis == "z" else x_peer(direction)
        copy = remote(piece(kind, src[0], src[1], half), piece(kind, dst[0], dst[1], half), device)
        copy.start()
        flows[kind, dst, half, axis, direction] = copy

    def along_z(kind, jx, k, direction):
        slots = SLOT_UP if direction > 0 else SLOT_DOWN
        if k < 4:
            half = None if k < 3 else (0 if direction > 0 else 1)
            send(kind, "z", direction, (jx, slots[k]), (jx, slots[k + 1]), half)

    def along_x(kind, jx, slot):
        if jx == 0:
            send(kind, "x", 1, (0, slot), (1, slot), None)
            send(kind, "x", -1, (0, slot), (2, slot), None)
        elif jx == 1:
            send(kind, "x", 1, (1, slot), (3, slot), 0)
        elif jx == 2:
            send(kind, "x", -1, (2, slot), (3, slot), 1)

    def got(kind, dst, half, axis, direction):
        flows[kind, dst, half, axis, direction].wait_recv()

    def arrive(kind, jx, dz):
        k = abs(dz)
        up = dz < 0
        slot = (SLOT_UP if up else SLOT_DOWN)[k]
        z_last = kind == "d" and k > 0 or kind == "u" and jx == 0
        if z_last:
            if k == 4:
                got(kind, (jx, 7), 0, "z", 1)
                got(kind, (jx, 7), 1, "z", -1)
            else:
                got(kind, (jx, slot), None, "z", 1 if up else -1)
                along_z(kind, jx, k, 1 if up else -1)
            if kind == "u":
                along_x(kind, 0, slot)
        else:
            if jx == 3:
                got(kind, (3, slot), 0, "x", 1)
                got(kind, (3, slot), 1, "x", -1)
            else:
                got(kind, (jx, slot), None, "x", 1 if jx == 1 else -1)
                along_x(kind, jx, slot)
            if kind == "d":
                along_z(kind, jx, 0, 1)
                along_z(kind, jx, 0, -1)

    along_z("u", 0, 0, 1)
    along_z("u", 0, 0, -1)
    along_x("d", 0, 0)
    along_x("u", 0, 0)
    along_z("d", 0, 0, 1)
    along_z("d", 0, 0, -1)

    x_mate = remote(x_buf.at[0], x_buf.at[1], mate)
    x_mate.start()
    x_partner = []
    for j in range(4):
        rows = pl.ds(128 * j, 128)
        copy = remote(x_buf.at[0, rows], x_buf.at[2, rows], partner)
        copy.start()
        x_partner.append(copy)
    x_pass = []

    bias_z = []
    for k in range(1, NZ):
        slot = SLOT_UP[k] if k <= 4 else SLOT_DOWN[NZ - k]
        copy = remote(bb.at[0, 0], bb.at[0, slot], z_peer(k))
        copy.start()
        bias_z.append(copy)
    bias_x = []

    def tally(first, last):
        def body(i, carry):
            delta = codes[...] - i * 256
            total = jnp.zeros((256, 256), F32)
            for part in range(4):
                row = lax.broadcasted_iota(jnp.int32, (256, 512), 0)
                hot = jnp.where(row == delta[:, 512 * part : 512 * (part + 1)], 1.0, 0.0).astype(BF)
                total = total + jnp.dot(hot, sv[512 * part : 512 * (part + 1), :], preferred_element_type=F32)
            for j in range(2):
                here = total[128 * j : 128 * (j + 1)]
                diagonal = lax.broadcasted_iota(jnp.int32, (128, 128), 0) == lax.broadcasted_iota(
                    jnp.int32, (128, 128), 1
                )
                count = jnp.sum(jnp.where(diagonal, here[:, 128:], 0.0), axis=0, keepdims=True)
                tt[2 * i + j, 0:128, :] = here[:, :128].astype(BF)
                tt[2 * i + j, 128:144, :] = count_rows(count[None], 1)[0].astype(BF)
            return carry

        lax.fori_loop(first, last, body, 0)

    def x_blocks(k):
        return pl.multiple_of(((x + k + NX) % NX) * NZ, NZ)

    rs = {}

    def add_into(base, count, others):
        def body(i, carry):
            total = tt[pl.ds(base + i, 1)].astype(F32)
            for ref in others:
                total = total + ref[pl.ds(i, 1)].astype(F32)
            tt[pl.ds(base + i, 1)] = tidy_block(total)
            return carry

        lax.fori_loop(0, count, body, 0)

    def reduce_1():
        far = x_blocks(2)
        rs["a+"] = remote(tt.at[pl.ds(far, 4)], ra.at[0], x_peer(1))
        rs["a-"] = remote(tt.at[pl.ds(far + 4, 4)], ra.at[1], x_peer(-1))
        rs["a+"].start()
        rs["a-"].start()

    def reduce_2():
        rs["a+"].wait_recv()
        rs["a-"].wait_recv()
        add_into(x_blocks(1), 4, [ra.at[0]])
        rs["b+"] = remote(tt.at[pl.ds(x_blocks(1), 8)], rb.at[0], x_peer(1))
        rs["b+"].start()
        add_into(x_blocks(-1) + 4, 4, [ra.at[1]])
        rs["b-"] = remote(tt.at[pl.ds(x_blocks(-1), 8)], rb.at[1], x_peer(-1))
        rs["b-"].start()

    def reduce_3():
        rs["b+"].wait_recv()
        rs["b-"].wait_recv()
        add_into(x_blocks(0), 8, [rb.at[0], rb.at[1]])
        for k in (4, 3, 5, 2, 6, 1, 7):
            rs["c", k] = remote(tt.at[x_blocks(0) + (z + k) % NZ], rc.at[k - 1], z_peer(k))
            rs["c", k].start()

    def reduce_4():
        for k in range(1, NZ):
            rs["c", k].wait_recv()
        total = tt[pl.ds(x_blocks(0) + z, 1)].astype(F32)
        for k in range(1, NZ):
            total = total + rc[k - 1 : k].astype(F32)
        ff[pl.ds(x_blocks(0) + z, 1)] = tidy_block(total)
        for k in (4, 3, 5, 2, 6, 1, 7):
            mine = ff.at[x_blocks(0) + z]
            rs["f", k] = remote(mine, mine, z_peer(k))
            rs["f", k].start()

    def gather_1():
        for k in range(1, NZ):
            rs["f", k].wait_recv()
        mine = ff.at[pl.ds(x_blocks(0), 8)]
        for k in (1, -1):
            rs["g", k] = remote(mine, mine, x_peer(k))
            rs["g", k].start()

    def gather_2():
        for k, half in ((1, 0), (-1, 1)):
            rs["g", k].wait_recv()
            part = ff.at[pl.ds(x_blocks(-k) + 4 * half, 4)]
            rs["h", k] = remote(part, part, x_peer(k))
            rs["h", k].start()

    def gather_3():
        rs["h", 1].wait_recv()
        rs["h", -1].wait_recv()

    def bias_of(h, first):
        lanes = lax.broadcasted_iota(jnp.int32, (1, 128), 1) // 32
        parts = []
        for jx in (first, first + 1):
            part = jnp.zeros((1, 128), F32)
            for i in range(4):
                part = jnp.where(lanes == i, bb[jx, 4 * h + i, 0:1, :], part)
            parts.append(part)
        return jnp.concatenate(parts, axis=1)

    def forward(g, b, finish=None):
        h, first = g // 2, 2 * (g % 2)
        bias = bias_of(h, first)
        up = gu[h, first : first + 2].reshape(256, 1024)
        down = gd[h, first : first + 2].reshape(256, 1024)

        def body(i, carry):
            rows = pl.ds(pl.multiple_of(256 * i, 256), 256)
            pre = lax.dot_general(
                x_buf[b, rows, :], up, (((1,), (1,)), ((), ())), preferred_element_type=F32
            )
            hidden = gelu(pre + bias).astype(BF)
            out = jnp.dot(hidden, down, preferred_element_type=F32)
            if g > 0:
                out = out + acc[b, rows, :]
            if finish is None:
                acc[b, rows, :] = out
            else:
                ps[finish, rows, :] = out.astype(BF)
            return carry

        lax.fori_loop(0, 2, body, 0)

    rounds = {}
    for dz in (0, -1, 1, -2, 2, -3, 3, 4):
        for jx in range(4):
            reach = abs(dz) + (0, 1, 1, 2)[jx]
            if reach:
                rounds.setdefault(reach, []).append((jx, dz))

    def do_round(r):
        for kind in ("u", "d"):
            for jx, dz in rounds[r]:
                arrive(kind, jx, dz)

    def bias_spread():
        for copy in bias_z:
            copy.wait_recv()
        for k, slot in ((1, 1), (-1, 2), (2, 3)):
            copy = remote(bb.at[0], bb.at[slot], x_peer(k))
            copy.start()
            bias_x.append(copy)

    def pass_rows(first, last):
        for j in range(first, last):
            x_partner[j].wait_recv()
            rows = pl.ds(128 * j, 128)
            copy = remote(x_buf.at[2, rows], x_buf.at[3, rows], mate)
            copy.start()
            x_pass.append(copy)

    load_s.wait()
    tally(0, 5)
    do_round(1)
    bias_spread()
    tally(5, 12)
    do_round(2)
    tally(12, 16)
    reduce_1()
    pass_rows(0, 2)
    do_round(3)
    pass_rows(2, 3)
    x_mate.wait_recv()
    for copy in bias_x:
        copy.wait_recv()
    forward(0, 0)
    reduce_2()
    forward(0, 1)
    do_round(4)
    pass_rows(3, 4)
    forward(1, 0)
    forward(1, 1)
    reduce_3()
    for copy in x_pass:
        copy.wait_recv()
    forward(0, 2)
    forward(0, 3)
    do_round(5)
    forward(1, 2)
    forward(1, 3)
    forward(2, 3)
    forward(2, 2)
    reduce_4()
    forward(2, 1)
    forward(2, 0)
    do_round(6)

    forward(3, 3, 0)
    to_mate_3 = remote(ps.at[0], pr.at[0], mate)
    to_mate_3.start()
    forward(3, 2)
    to_mate_3.wait_recv()
    to_partner = []
    for j in range(4):
        rows = pl.ds(128 * j, 128)
        ps[1, rows, :] = (acc[2, rows, :] + pr[0, rows, :].astype(F32)).astype(BF)
        copy = remote(ps.at[1, rows], pr.at[2, rows], partner)
        copy.start()
        to_partner.append(copy)
    forward(3, 1, 2)
    to_mate_1 = remote(ps.at[2], pr.at[1], mate)
    to_mate_1.start()
    forward(3, 0)
    gather_1()
    to_mate_1.wait_recv()

    ends = [lengths[0, 0, 0]]
    for p in range(1, 4):
        ends.append(ends[-1] + lengths[0, 0, p])
    row8 = lax.broadcasted_iota(jnp.int32, (8, 1), 0)
    opening = jnp.full((8, 1), 0, jnp.int32)
    ending = jnp.full((8, 1), 0, jnp.int32)
    size = jnp.full((8, 1), 1, jnp.int32)
    for p in range(4):
        opening = jnp.where(row8 == p, ends[p] - lengths[0, 0, p], opening)
        ending = jnp.where(row8 == p, ends[p], ending)
        size = jnp.where(row8 == p, lengths[0, 0, p], size)

    pooled[...] = jnp.zeros((8, 1024), F32)
    for j in range(4):
        to_partner[j].wait_recv()
        rows = pl.ds(128 * j, 128)
        resid = (
            x_buf[0, rows, :].astype(F32)
            + (acc[0, rows, :] + pr[1, rows, :].astype(F32) + pr[2, rows, :].astype(F32))
            + down_bias[...]
        )
        center = resid - jnp.mean(resid, axis=-1, keepdims=True)
        spread = jnp.mean(center * center, axis=-1, keepdims=True)
        layer_out = (center * lax.rsqrt(spread + 1e-12) * ln_gain[...] + ln_bias[...]).astype(BF)
        place = lax.broadcasted_iota(jnp.int32, (8, 128), 1) + 128 * j
        member = jnp.where((place >= opening) & (place < ending), 1.0, 0.0).astype(BF)
        pooled[...] += jnp.dot(member, layer_out, preferred_element_type=F32)
        if j == 1:
            gather_2()
    mean = pooled[...] / size.astype(F32)
    scaling = lax.rsqrt(jnp.mean(mean * mean, axis=-1, keepdims=True) + 1e-06)
    embedded = (mean * scaling).astype(BF).astype(F32)
    for i in range(NS):
        em[i] = embedded[:, 128 * i : 128 * (i + 1)]

    to_owner = []
    for k in range(1, NS):
        copy = remote(em.at[(s + k) % NS], er.at[s], s_peer(k))
        copy.start()
        to_owner.append(copy)
    er[pl.ds(s, 1)] = em[pl.ds(s, 1)]
    gather_3()
    save_f = local(ff, f_out)
    for copy in to_owner:
        copy.wait_recv()
    low = lax.broadcasted_iota(jnp.int32, (8, 128), 0) < 4
    tiles = [jnp.where(low, er[2 * i], pltpu.roll(er[2 * i + 1], 4, 0)) for i in range(4)]
    ee[x, z] = jnp.concatenate(tiles, axis=0).astype(BF)

    e_copies = []
    for k in (4, 3, 5, 2, 6, 1, 7):
        copy = remote(ee.at[x, z], ee.at[x, z], z_peer(k))
        copy.start()
        e_copies.append(copy)
    for copy in e_copies:
        copy.wait_recv()
    e_copies = []
    for k in (2, 1, 3):
        copy = remote(ee.at[x], ee.at[x], x_peer(k))
        copy.start()
        e_copies.append(copy)
    for copy in e_copies:
        copy.wait_recv()
    saves = [local(ee.at[i], e_out.at[:, i]) for i in range(NX)]
    for copy in started:
        copy.wait_send()
    save_f.wait()
    for copy in saves:
        copy.wait()


def update_kernel(e_all, new_codes, table, centroids, embeds, updated, right):
    i = pl.program_id(0)

    @pl.when(i == 0)
    def _():
        right[0:1024, 0:128] = e_all[...]
        right[0:1024, 128:256] = jnp.ones((1024, 128), BF)
        lanes = lax.broadcasted_iota(jnp.int32, (128, 256), 1)
        right[1024:1152, :] = jnp.where(lanes >= 128, 256.0, 0.0).astype(BF)
        right[1152:1280, :] = jnp.where(lanes >= 128, 1.0, 0.0).astype(BF)
        mine = pl.multiple_of(lax.axis_index("dp") * 32, 32)
        embeds[...] = e_all[pl.ds(mine, 32), :]

    diagonal = lax.broadcasted_iota(jnp.int32, (128, 128), 0) == lax.broadcasted_iota(
        jnp.int32, (128, 128), 1
    )
    row = lax.broadcasted_iota(jnp.int32, (128, 1024), 0)
    for j in range(4):
        rows = pl.ds(128 * j, 128)
        delta = new_codes[...] - (i * 512 + 128 * j)
        hot = jnp.where(row == delta, 1.0, 0.0).astype(BF)
        high = jnp.where(diagonal, table[j, 128:129, :].astype(F32), 0.0).astype(BF)
        low = jnp.where(diagonal, table[j, 129:130, :].astype(F32), 0.0).astype(BF)
        left = jnp.concatenate([hot, high, low], axis=1)
        new = jnp.dot(left, right[...], preferred_element_type=F32)
        total = table[j, 0:128, :].astype(F32) + new[:, :128] + centroids[0, rows, :]
        updated[0, rows, :] = total / (new[:, 128:] + 1.0)


def on_device(
    tokens, lengths, w_up, up_bias, w_down, down_bias, ln_gain, ln_bias, stored, stored_codes, new_codes, centroids
):
    vmem = pl.BlockSpec(memory_space=pltpu.VMEM)
    smem = pl.BlockSpec(memory_space=pltpu.SMEM)
    hbm = pl.BlockSpec(memory_space=pl.ANY)
    e_all, table = pl.pallas_call(
        layer_kernel,
        out_shape=(
            jax.ShapeDtypeStruct((NZ, NX, 32, 128), BF),
            jax.ShapeDtypeStruct((32, 144, 128), BF),
        ),
        in_specs=[hbm, hbm, hbm, hbm, smem, vmem, vmem, vmem, vmem, vmem],
        out_specs=(hbm, hbm),
        scratch_shapes=[
            pltpu.VMEM((4, 512, 1024), BF),
            pltpu.VMEM((2, 4, 4, 32, 1024), BF),
            pltpu.VMEM((2, 4, 4, 32, 1024), BF),
            pltpu.VMEM((4, 512, 1024), F32),
            pltpu.VMEM((3, 512, 1024), BF),
            pltpu.VMEM((3, 512, 1024), BF),
            pltpu.VMEM((2048, 256), BF),
            pltpu.VMEM((32, 144, 128), BF),
            pltpu.VMEM((2, 4, 144, 128), BF),
            pltpu.VMEM((2, 8, 144, 128), BF),
            pltpu.VMEM((7, 144, 128), BF),
            pltpu.VMEM((32, 144, 128), BF),
            pltpu.VMEM((4, 8, 8, 128), F32),
            pltpu.VMEM((8, 8, 128), F32),
            pltpu.VMEM((8, 8, 128), F32),
            pltpu.VMEM((NX, NZ, 32, 128), BF),
            pltpu.VMEM((8, 1024), F32),
            pltpu.SemaphoreType.DMA((256,)),
            pltpu.SemaphoreType.DMA((256,)),
            pltpu.SemaphoreType.DMA((16,)),
        ],
        compiler_params=pltpu.CompilerParams(
            collective_id=0, has_side_effects=True, vmem_limit_bytes=52 * 1024 * 1024
        ),
    )(
        tokens, w_up, w_down, stored, lengths, up_bias.reshape(1, 128), down_bias.reshape(1, 1024),
        ln_gain.reshape(1, 1024), ln_bias.reshape(1, 1024), stored_codes,
    )
    embeds, updated = pl.pallas_call(
        update_kernel,
        grid=(8,),
        out_shape=(
            jax.ShapeDtypeStruct((32, 128), BF),
            jax.ShapeDtypeStruct((1, 4096, 128), F32),
        ),
        in_specs=[
            pl.BlockSpec((1024, 128), lambda i: (0, 0)),
            pl.BlockSpec((1, 1024), lambda i: (0, 0)),
            pl.BlockSpec((4, 144, 128), lambda i: (i, 0, 0)),
            pl.BlockSpec((1, 512, 128), lambda i: (0, i, 0)),
        ],
        out_specs=(
            pl.BlockSpec((32, 128), lambda i: (0, 0)),
            pl.BlockSpec((1, 512, 128), lambda i: (0, i, 0)),
        ),
        scratch_shapes=[pltpu.VMEM((1280, 256), BF)],
        compiler_params=pltpu.CompilerParams(vmem_limit_bytes=32 * 1024 * 1024),
    )(e_all.reshape(1024, 128), new_codes, table, centroids)
    return embeds, updated


def solution(mesh):
    return jax.shard_map(
        on_device,
        mesh=mesh,
        in_specs=(
            P(("dp", "sub"), None),
            P("dp", "sub", None),
            P("dp", None),
            P("dp"),
            P("dp", None),
            P(),
            P(),
            P(),
            P("dp", "sub"),
            P("sub", "dp"),
            P("sub", None),
            P("sub", None, None),
        ),
        out_specs=(P("dp", "sub"), P("sub", None, None)),
        check_vma=False,
    )
```

```python
import functools

import jax
import jax.numpy as jnp
from jax import lax
from jax.experimental import pallas as pl
from jax.experimental.pallas import tpu as pltpu
from jax.sharding import PartitionSpec as P

MESH = pl.DeviceIdType.MESH
NX, NZ, NS = 4, 8, 8
BF, F32 = jnp.bfloat16, jnp.float32

GELU_P = (
    0.7978849411010742,
    0.03633308410644531,
    -3.259497316321358e-05,
    -5.530619455385022e-05,
    3.964744792028796e-06,
    -1.322633664813111e-07,
    1.7561715415226331e-09,
)
GELU_CAP = 30.0

SLOT_UP = (0, 1, 3, 5, 7)
SLOT_DOWN = (0, 2, 4, 6, 7)


ORDER = (
    101, 111, 340, 341, 354, 370, 201, 211, 352, 353, 355, 350, 313, 303, 0, 1, 2, 3, 4, 340, 342, 221, 231, 341,
    343, 241, 251, 370, 371, 350, 5, 101, 102, 302, 312, 111, 112, 304, 314, 201, 202, 211, 212, 313, 333, 303, 323,
    6, 7, 373, 372, 342, 343, 261, 271, 231, 232, 221, 222, 251, 252, 241, 242, 333, 323, 371, 354, 358, 302, 322,
    102, 103, 301, 311, 112, 113, 305, 315, 202, 203, 212, 213, 352, 356, 353, 357, 355, 359, 312, 332, 304, 324,
    314, 334, 358, 261, 262, 271, 272, 372, 373, 9, 375, 8, 374, 356, 357, 359, 222, 223, 232, 233, 322, 252, 253,
    242, 243, 324, 332, 334, 301, 321, 23, 213, 214, 103, 104, 300, 310, 113, 114, 316, 306, 203, 204, 311, 331,
    305, 325, 315, 335, 22, 272, 273, 262, 263, 21, 223, 224, 233, 234, 20, 321, 243, 244, 253, 254, 104, 214, 204,
    114, 307, 317, 325, 273, 274, 263, 264, 331, 27, 335, 224, 234, 244, 254, 26, 300, 320, 306, 326, 25, 274, 316,
    336, 264, 310, 330, 24, 307, 327, 317, 337, 31, 375, 374, 10, 380, 29, 320, 326, 30, 336, 330, 327, 337, 28, 46,
    364, 47, 365, 44, 45, 42, 366, 43, 367, 40, 41, 364, 51, 361, 50, 360, 380, 11, 381, 365, 52, 362, 53, 363, 366,
    367, 381, 376, 377, 361, 360, 54, 55, 362, 363, 56, 57, 58, 382, 382, 59, 400, 393, 395, 392, 396, 394, 391,
    397, 376, 378, 377, 379, 400, 391, 401, 397, 407, 392, 402, 396, 406, 393, 403, 395, 405, 394, 404, 401, 407,
    402, 406, 403, 405, 404, 378, 379,
)


def gelu(p):
    t = jnp.minimum(p * p, GELU_CAP)
    q = jnp.full_like(t, GELU_P[-1])
    for coefficient in GELU_P[-2::-1]:
        q = q * t + coefficient
    half = 0.5 * p
    return half + half * jnp.tanh(p * q)


def tidy_block(total):
    n = total.shape[0]
    count = 256.0 * total[:, 128:129, :] + total[:, 129:130, :]
    return jnp.concatenate([total[:, :128, :], count_rows(count, n)], axis=1).astype(BF)


def count_rows(count, n):
    high = jnp.floor(count * (1.0 / 256.0))
    low = count - 256.0 * high
    row = lax.broadcasted_iota(jnp.int32, (n, 16, 128), 1)
    return jnp.where(row == 0, high, jnp.where(row == 1, low, 0.0))


def layer_kernel(
    tokens, w_up, w_down, stored, lengths_in, up_bias_in, down_bias_in, ln_gain_in, ln_bias_in, codes_in,
    e_out, f_out, lengths, up_bias, down_bias, ln_gain, ln_bias, codes,
    x_buf, gu, gd, acc, ps, pr, sv, tt, ra, rb, rc, ff, bb, em, er, ee, pooled,
    send_sem, recv_sem, local_sem,
):
    dp, s = lax.axis_index("dp"), lax.axis_index("sub")
    z, x, core = dp // NX, dp % NX, s % 2
    quarter = ((s // 2) % 2) * 2 + core

    def z_peer(k):
        return (((z + k + NZ) % NZ) * NX + x, s)

    def x_peer(k):
        return (z * NX + (x + k + NX) % NX, s)

    def s_peer(k):
        return (dp, (s + k) % NS)

    mate = (dp, s + 1 - 2 * core)
    partner = (dp, (s + 2 * core - 1 + NS) % NS)

    used = [0]
    sent = {}

    def remote(src, dst, device, arrival):
        return pltpu.make_async_remote_copy(
            src_ref=src, dst_ref=dst, send_sem=send_sem, recv_sem=arrival,
            device_id=device, device_id_type=MESH,
        )

    def local(src, dst):
        i = used[0]
        used[0] += 1
        copy = pltpu.make_async_copy(src, dst, local_sem.at[i])
        copy.start()
        return copy

    barrier = pltpu.get_barrier_semaphore()
    peers = [z_peer(k) for k in range(1, NZ)] + [x_peer(k) for k in range(1, NX)] + [s_peer(k) for k in range(1, NS)]
    for device in peers:
        pl.semaphore_signal(barrier, inc=1, device_id=device, device_id_type=MESH)

    row0 = pl.multiple_of(quarter * 32, 32)
    load_up = local(w_up.at[pl.ds(row0, 32)], gu.at[0, 0, 0])
    load_down = local(w_down.at[pl.ds(row0, 32)], gd.at[0, 0, 0])
    load_x = local(tokens, x_buf.at[0])
    load_bias = local(up_bias_in, up_bias)
    load_codes = local(codes_in, codes)
    load_s = local(stored, sv.at[:, pl.ds(0, 128)])
    load_rest = [local(lengths_in, lengths), local(down_bias_in, down_bias), local(ln_gain_in, ln_gain), local(ln_bias_in, ln_bias)]
    load_bias.wait()
    lane = lax.broadcasted_iota(jnp.int32, (8, 128), 1)
    own_bias = jnp.where(lane // 32 == quarter, jnp.broadcast_to(up_bias[...].astype(F32), (8, 128)), 0.0)
    own_bias = own_bias + pltpu.roll(own_bias, 64, 1)
    bb[0, 0] = own_bias + pltpu.roll(own_bias, 32, 1)
    sv[:, 128:256] = jnp.ones((2048, 128), BF)

    load_up.wait()
    load_down.wait()
    load_x.wait()
    pl.semaphore_wait(barrier, len(peers))

    copies = {}

    def piece(buffer, jx, slot, half=None):
        ref = buffer.at[slot // 4, jx, slot % 4]
        return ref if half is None else ref.at[pl.ds(16 * half, 16)]

    ways = ((1, SLOT_UP, 0), (-1, SLOT_DOWN, 1))
    for way, slots, half in ways:
        for k in range(1, 5):
            part = half if k == 4 else None
            copies[100 + 10 * half + k] = [
                (piece(gu, 0, slots[k - 1], part), piece(gu, 0, slots[k], part), z_peer(way))
            ]
            for jx in range(4):
                copies[200 + 20 * jx + 10 * half + k] = [
                    (piece(gd, jx, slots[k - 1], part), piece(gd, jx, slots[k], part), z_peer(way))
                ]
        near = 1 if way > 0 else 2
        for dz in range(-3, 5):
            slot = SLOT_UP[-dz] if dz < 0 else SLOT_DOWN[dz]
            copies[303 + 10 * half + dz] = [(piece(gu, 0, slot), piece(gu, near, slot), x_peer(way))]
            copies[323 + 10 * half + dz] = [(piece(gu, near, slot, half), piece(gu, 3, slot, half), x_peer(way))]
        copies[340 + half] = [(piece(gd, 0, 0), piece(gd, near, 0), x_peer(way))]
        copies[342 + half] = [(piece(gd, near, 0, half), piece(gd, 3, 0, half), x_peer(way))]

    def part_of(ref, j, size):
        return ref.at[pl.ds(size * j, size)]

    copies[350] = [(x_buf.at[0], x_buf.at[1], mate)]
    for j in range(4):
        copies[352 + j] = [(part_of(x_buf.at[0], j, 128), part_of(x_buf.at[2], j, 128), partner)]
        copies[356 + j] = [(part_of(x_buf.at[2], j, 128), part_of(x_buf.at[3], j, 128), mate)]
        copies[360 + j] = [(part_of(ps.at[1], j, 128), part_of(pr.at[2], j, 128), partner)]
    for i in range(2):
        copies[364 + i] = [(part_of(ps.at[0], i, 256), part_of(pr.at[0], i, 256), mate)]
        copies[366 + i] = [(part_of(ps.at[2], i, 256), part_of(pr.at[1], i, 256), mate)]
    copies[370] = [
        (bb.at[0, 0], bb.at[0, SLOT_UP[k] if k <= 4 else SLOT_DOWN[NZ - k]], z_peer(k)) for k in range(1, NZ)
    ]
    copies[371] = [(bb.at[0], bb.at[slot], x_peer(k)) for k, slot in ((1, 1), (-1, 2), (2, 3))]

    def x_blocks(k):
        return pl.multiple_of(((x + k + NX) % NX) * NZ, NZ)

    far, own = x_blocks(2), x_blocks(0)
    for way, slots, half in ways:
        copies[372 + half] = [(tt.at[pl.ds(far + 4 * half, 4)], ra.at[half], x_peer(way))]
        copies[374 + half] = [(tt.at[pl.ds(x_blocks(way), 8)], rb.at[half], x_peer(way))]
        copies[376 + half] = [(ff.at[pl.ds(own, 8)], ff.at[pl.ds(own, 8)], x_peer(way))]
        passed = ff.at[pl.ds(x_blocks(-way) + 4 * half, 4)]
        copies[378 + half] = [(passed, passed, x_peer(way))]
    copies[380] = [(tt.at[own + (z + k) % NZ], rc.at[k - 1], z_peer(k)) for k in range(1, NZ)]
    copies[381] = [(ff.at[own + z], ff.at[own + z], z_peer(k)) for k in range(1, NZ)]
    copies[382] = [(em.at[(s + k) % NS], er.at[s], s_peer(k)) for k in range(1, NS)]
    for k in range(NZ):
        row = (z - k + NZ) % NZ
        if k:
            copies[390 + k] = [(ee.at[x, z], ee.at[x, z], z_peer(k))]
        copies[400 + k] = [(ee.at[x, row], ee.at[x, row], x_peer(j)) for j in (2, 1, 3)]

    compute = {}

    def tally(first, last):
        def body(i, carry):
            delta = codes[...] - i * 256
            total = jnp.zeros((256, 256), F32)
            for part in range(4):
                row = lax.broadcasted_iota(jnp.int32, (256, 512), 0)
                hot = jnp.where(row == delta[:, 512 * part : 512 * (part + 1)], 1.0, 0.0).astype(BF)
                total = total + jnp.dot(hot, sv[512 * part : 512 * (part + 1), :], preferred_element_type=F32)
            for j in range(2):
                here = total[128 * j : 128 * (j + 1)]
                diagonal = lax.broadcasted_iota(jnp.int32, (128, 128), 0) == lax.broadcasted_iota(
                    jnp.int32, (128, 128), 1
                )
                count = jnp.sum(jnp.where(diagonal, here[:, 128:], 0.0), axis=0, keepdims=True)
                tt[2 * i + j, 0:128, :] = here[:, :128].astype(BF)
                tt[2 * i + j, 128:144, :] = count_rows(count[None], 1)[0].astype(BF)
            return carry

        lax.fori_loop(first, last, body, 0)

    for i in range(8):
        compute[i] = functools.partial(tally, 2 * i, 2 * i + 2)

    def add_into(base, count, others):
        def body(i, carry):
            total = tt[pl.ds(base + i, 1)].astype(F32)
            for ref in others:
                total = total + ref[pl.ds(i, 1)].astype(F32)
            tt[pl.ds(base + i, 1)] = tidy_block(total)
            return carry

        lax.fori_loop(0, count, body, 0)

    compute[8] = lambda: add_into(x_blocks(1), 4, [ra.at[0]])
    compute[9] = lambda: add_into(x_blocks(-1) + 4, 4, [ra.at[1]])
    compute[10] = lambda: add_into(own, 8, [rb.at[0], rb.at[1]])

    def add_z():
        total = tt[pl.ds(own + z, 1)].astype(F32)
        for k in range(1, NZ):
            total = total + rc[k - 1 : k].astype(F32)
        ff[pl.ds(own + z, 1)] = tidy_block(total)

    compute[11] = add_z

    def bias_of(h, first):
        lanes = lax.broadcasted_iota(jnp.int32, (1, 128), 1) // 32
        parts = []
        for jx in (first, first + 1):
            part = jnp.zeros((1, 128), F32)
            for i in range(4):
                part = jnp.where(lanes == i, bb[jx, 4 * h + i, 0:1, :], part)
            parts.append(part)
        return jnp.concatenate(parts, axis=1)

    def forward_tile(g, b, i, finish=None):
        h, first = g // 2, 2 * (g % 2)
        rows = pl.ds(256 * i, 256)
        up = gu[h, first : first + 2].reshape(256, 1024)
        down = gd[h, first : first + 2].reshape(256, 1024)
        pre = lax.dot_general(x_buf[b, rows, :], up, (((1,), (1,)), ((), ())), preferred_element_type=F32)
        hidden = gelu(pre + bias_of(h, first)).astype(BF)
        out = jnp.dot(hidden, down, preferred_element_type=F32)
        if g > 0:
            out = out + acc[b, rows, :]
        if finish is None:
            acc[b, rows, :] = out
        else:
            ps[finish, rows, :] = out.astype(BF)

    def forward(g, b):
        for i in range(2):
            forward_tile(g, b, i)

    for b in range(4):
        for g in range(3):
            compute[20 + 4 * g + b] = functools.partial(forward, g, b)
        for i in range(2):
            compute[40 + 2 * b + i] = functools.partial(forward_tile, 3, b, i, {3: 0, 1: 2}.get(b))

    def add_mate(j):
        rows = pl.ds(128 * j, 128)
        ps[1, rows, :] = (acc[2, rows, :] + pr[0, rows, :].astype(F32)).astype(BF)

    def place_of_passages():
        ends = [lengths[0, 0, 0]]
        for p in range(1, 4):
            ends.append(ends[-1] + lengths[0, 0, p])
        row8 = lax.broadcasted_iota(jnp.int32, (8, 1), 0)
        opening = jnp.full((8, 1), 0, jnp.int32)
        ending = jnp.full((8, 1), 0, jnp.int32)
        size = jnp.full((8, 1), 1, jnp.int32)
        for p in range(4):
            opening = jnp.where(row8 == p, ends[p] - lengths[0, 0, p], opening)
            ending = jnp.where(row8 == p, ends[p], ending)
            size = jnp.where(row8 == p, lengths[0, 0, p], size)
        return opening, ending, size

    def norm_rows(j):
        if j == 0:
            pooled[...] = jnp.zeros((8, 1024), F32)
        opening, ending, _ = place_of_passages()
        rows = pl.ds(128 * j, 128)
        resid = (
            x_buf[0, rows, :].astype(F32)
            + (acc[0, rows, :] + pr[1, rows, :].astype(F32) + pr[2, rows, :].astype(F32))
            + down_bias[...]
        )
        center = resid - jnp.mean(resid, axis=-1, keepdims=True)
        spread = jnp.mean(center * center, axis=-1, keepdims=True)
        layer_out = (center * lax.rsqrt(spread + 1e-12) * ln_gain[...] + ln_bias[...]).astype(BF)
        place = lax.broadcasted_iota(jnp.int32, (8, 128), 1) + 128 * j
        member = jnp.where((place >= opening) & (place < ending), 1.0, 0.0).astype(BF)
        pooled[...] += jnp.dot(member, layer_out, preferred_element_type=F32)

    for j in range(4):
        compute[50 + j] = functools.partial(add_mate, j)
        compute[54 + j] = functools.partial(norm_rows, j)

    def embed():
        _, _, size = place_of_passages()
        mean = pooled[...] / size.astype(F32)
        scaling = lax.rsqrt(jnp.mean(mean * mean, axis=-1, keepdims=True) + 1e-06)
        embedded = (mean * scaling).astype(BF).astype(F32)
        for i in range(NS):
            em[i] = embedded[:, 128 * i : 128 * (i + 1)]
        er[pl.ds(s, 1)] = em[pl.ds(s, 1)]

    def own_rows():
        low = lax.broadcasted_iota(jnp.int32, (8, 128), 0) < 4
        tiles = [jnp.where(low, er[2 * i], pltpu.roll(er[2 * i + 1], 4, 0)) for i in range(4)]
        ee[x, z] = jnp.concatenate(tiles, axis=0).astype(BF)

    compute[58] = embed
    compute[59] = own_rows

    landing = {
        370: bb.at[0, pl.ds(1, 7)], 371: bb.at[pl.ds(1, 3)], 380: rc, 381: rc, 382: er.at[pl.ds(1, 7)],
    }
    load_codes.wait()
    load_s.wait()
    for copy in load_rest:
        copy.wait()
    running = {}
    for name in ORDER:
        if name in running:
            running[name].wait_recv()
        elif name in copies:
            arrival = recv_sem.at[len(running)]
            for source, target, device in copies[name]:
                copy = remote(source, target, device, arrival)
                copy.start()
            if len(copies[name]) > 1:
                whole = landing.get(name)
                if whole is None:
                    whole = ee.at[0, pl.ds(0, 3)]
                copy = remote(whole, whole, device, arrival)
            running[name] = copy
        else:
            compute[name]()
    saves = [local(ff, f_out)] + [local(ee.at[i], e_out.at[:, i]) for i in range(NX)]
    total = 0
    for ends in copies.values():
        for source, _, _ in ends:
            total += source.size * source.dtype.itemsize
    for whole in (acc, x_buf, sv):
        size = whole.size * whole.dtype.itemsize
        for _ in range(total // size):
            pltpu.make_async_copy(whole, whole, send_sem).wait()
        total %= size
    rows = pl.ds(0, total // 32768 * 16)
    pltpu.make_async_copy(ps.at[0, rows], ps.at[0, rows], send_sem).wait()
    if total % 32768:
        tiles = pl.ds(0, total % 32768 // 4096)
        pltpu.make_async_copy(er.at[tiles], er.at[tiles], send_sem).wait()
    for copy in saves:
        copy.wait()


def update_kernel(
    e_in, codes_in, table_in, centroids_in, embeds, updated,
    e_all, new_codes, table, centroids, result, right, load_sem, save_sem,
):
    def load(i, source, target):
        copy = pltpu.make_async_copy(source, target, load_sem.at[i])
        copy.start()
        return copy

    first = [load(0, codes_in, new_codes), load(1, e_in, e_all)]
    parts = []
    for i in range(8):
        blocks, rows = pl.ds(4 * i, 4), pl.ds(512 * i, 512)
        parts.append(
            [
                load(2 + 2 * i, table_in.at[blocks], table.at[blocks]),
                load(3 + 2 * i, centroids_in.at[0, rows], centroids.at[rows]),
            ]
        )
    right[0:1024, 128:256] = jnp.ones((1024, 128), BF)
    lanes = lax.broadcasted_iota(jnp.int32, (128, 256), 1)
    right[1024:1152, :] = jnp.where(lanes >= 128, 256.0, 0.0).astype(BF)
    right[1152:1280, :] = jnp.where(lanes >= 128, 1.0, 0.0).astype(BF)
    diagonal = lax.broadcasted_iota(jnp.int32, (128, 128), 0) == lax.broadcasted_iota(
        jnp.int32, (128, 128), 1
    )
    row = lax.broadcasted_iota(jnp.int32, (128, 1024), 0)
    for copy in first:
        copy.wait()
    right[0:1024, 0:128] = e_all[...]
    mine = pl.multiple_of(lax.axis_index("dp") * 32, 32)
    save_own = pltpu.make_async_copy(e_all.at[pl.ds(mine, 32)], embeds, load_sem.at[0])
    save_own.start()
    saves = []
    for i in range(8):
        for copy in parts[i]:
            copy.wait()
        for j in range(4 * i, 4 * i + 4):
            rows = pl.ds(128 * j, 128)
            hot = jnp.where(row == new_codes[...] - 128 * j, 1.0, 0.0).astype(BF)
            high = jnp.where(diagonal, table[j, 128:129, :].astype(F32), 0.0).astype(BF)
            low = jnp.where(diagonal, table[j, 129:130, :].astype(F32), 0.0).astype(BF)
            left = jnp.concatenate([hot, high, low], axis=1)
            new = jnp.dot(left, right[...], preferred_element_type=F32)
            total = table[j, 0:128, :].astype(F32) + new[:, :128] + centroids[rows, :]
            result[rows, :] = total / (new[:, 128:] + 1.0)
        rows = pl.ds(512 * i, 512)
        copy = pltpu.make_async_copy(result.at[rows], updated.at[0, rows], save_sem.at[i])
        copy.start()
        saves.append(copy)
    save_own.wait()
    for copy in saves:
        copy.wait()


def on_device(
    tokens, lengths, w_up, up_bias, w_down, down_bias, ln_gain, ln_bias, stored, stored_codes, new_codes, centroids
):
    hbm = pl.BlockSpec(memory_space=pltpu.HBM)
    e_all, table = pl.pallas_call(
        layer_kernel,
        out_shape=(
            jax.ShapeDtypeStruct((NZ, NX, 32, 128), BF),
            jax.ShapeDtypeStruct((32, 144, 128), BF),
        ),
        in_specs=[hbm, hbm, hbm, hbm, hbm, hbm, hbm, hbm, hbm, hbm],
        out_specs=(hbm, hbm),
        scratch_shapes=[
            pltpu.SMEM((1, 1, 4), jnp.int32),
            pltpu.VMEM((1, 128), BF),
            pltpu.VMEM((1, 1024), F32),
            pltpu.VMEM((1, 1024), F32),
            pltpu.VMEM((1, 1024), F32),
            pltpu.VMEM((1, 2048), jnp.int32),
            pltpu.VMEM((4, 512, 1024), BF),
            pltpu.VMEM((2, 4, 4, 32, 1024), BF),
            pltpu.VMEM((2, 4, 4, 32, 1024), BF),
            pltpu.VMEM((4, 512, 1024), F32),
            pltpu.VMEM((3, 512, 1024), BF),
            pltpu.VMEM((3, 512, 1024), BF),
            pltpu.VMEM((2048, 256), BF),
            pltpu.VMEM((32, 144, 128), BF),
            pltpu.VMEM((2, 4, 144, 128), BF),
            pltpu.VMEM((2, 8, 144, 128), BF),
            pltpu.VMEM((7, 144, 128), BF),
            pltpu.VMEM((32, 144, 128), BF),
            pltpu.VMEM((4, 8, 8, 128), F32),
            pltpu.VMEM((8, 8, 128), F32),
            pltpu.VMEM((8, 8, 128), F32),
            pltpu.VMEM((NX, NZ, 32, 128), BF),
            pltpu.VMEM((8, 1024), F32),
            pltpu.SemaphoreType.DMA,
            pltpu.SemaphoreType.DMA((121,)),
            pltpu.SemaphoreType.DMA((16,)),
        ],
        compiler_params=pltpu.CompilerParams(
            collective_id=0, has_side_effects=True, vmem_limit_bytes=64 * 1024 * 1024
        ),
    )(
        tokens, w_up, w_down, stored, lengths, up_bias.reshape(1, 128), down_bias.reshape(1, 1024),
        ln_gain.reshape(1, 1024), ln_bias.reshape(1, 1024), stored_codes,
    )
    embeds, updated = pl.pallas_call(
        update_kernel,
        out_shape=(
            jax.ShapeDtypeStruct((32, 128), BF),
            jax.ShapeDtypeStruct((1, 4096, 128), F32),
        ),
        in_specs=[hbm, hbm, hbm, hbm],
        out_specs=(hbm, hbm),
        scratch_shapes=[
            pltpu.VMEM((1024, 128), BF),
            pltpu.VMEM((1, 1024), jnp.int32),
            pltpu.VMEM((32, 144, 128), BF),
            pltpu.VMEM((4096, 128), F32),
            pltpu.VMEM((4096, 128), F32),
            pltpu.VMEM((1280, 256), BF),
            pltpu.SemaphoreType.DMA((18,)),
            pltpu.SemaphoreType.DMA((8,)),
        ],
        compiler_params=pltpu.CompilerParams(vmem_limit_bytes=64 * 1024 * 1024),
    )(e_all.reshape(1024, 128), new_codes, table, centroids)
    return embeds, updated


def solution(mesh):
    return jax.shard_map(
        on_device,
        mesh=mesh,
        in_specs=(
            P(("dp", "sub"), None),
            P("dp", "sub", None),
            P("dp", None),
            P("dp"),
            P("dp", None),
            P(),
            P(),
            P(),
            P("dp", "sub"),
            P("sub", "dp"),
            P("sub", None),
            P("sub", None, None),
        ),
        out_specs=(P("dp", "sub"), P("sub", None, None)),
        check_vma=False,
    )
```

```python
import functools

import jax
import jax.numpy as jnp
from jax import lax
from jax.experimental import pallas as pl
from jax.experimental.pallas import tpu as pltpu
from jax.sharding import PartitionSpec as P

MESH = pl.DeviceIdType.MESH
NX, NZ, NS = 4, 8, 8
BF, F32 = jnp.bfloat16, jnp.float32

GELU_P = (
    0.7978849411010742,
    0.03633308410644531,
    -3.259497316321358e-05,
    -5.530619455385022e-05,
    3.964744792028796e-06,
    -1.322633664813111e-07,
    1.7561715415226331e-09,
)
GELU_CAP = 30.0

SLOT_UP = (0, 1, 3, 5, 7)
SLOT_DOWN = (0, 2, 4, 6, 7)


ORDER = (
    101, 111, 340, 341, 354, 370, 201, 211, 352, 353, 355, 350, 313, 303, 0, 1, 2, 3, 4, 340, 342, 221, 231, 341,
    343, 241, 251, 370, 371, 350, 5, 101, 102, 302, 312, 111, 112, 304, 314, 201, 202, 211, 212, 313, 333, 303, 323,
    6, 7, 373, 372, 342, 343, 261, 271, 231, 232, 221, 222, 251, 252, 241, 242, 333, 323, 371, 354, 358, 302, 322,
    102, 103, 301, 311, 112, 113, 305, 315, 202, 203, 212, 213, 352, 356, 353, 357, 355, 359, 312, 332, 304, 324,
    314, 334, 358, 261, 262, 271, 272, 372, 373, 9, 375, 8, 374, 356, 357, 359, 222, 223, 232, 233, 322, 252, 253,
    242, 243, 324, 332, 334, 301, 321, 23, 213, 214, 103, 104, 300, 310, 113, 114, 316, 306, 203, 204, 311, 331,
    305, 325, 315, 335, 22, 272, 273, 262, 263, 21, 223, 224, 233, 234, 20, 321, 243, 244, 253, 254, 104, 214, 204,
    114, 307, 317, 325, 273, 274, 263, 264, 331, 27, 335, 224, 234, 244, 254, 26, 300, 320, 306, 326, 25, 274, 316,
    336, 264, 310, 330, 24, 307, 327, 317, 337, 31, 375, 374, 10, 380, 320, 326, 30, 336, 330, 327, 337, 46, 364,
    47, 365, 44, 364, 50, 360, 51, 361, 45, 365, 52, 362, 53, 363, 29, 42, 366, 43, 367, 380, 11, 381, 28, 40, 41,
    366, 367, 360, 54, 361, 55, 381, 376, 377, 362, 56, 363, 57, 58, 382, 382, 59, 393, 395, 392, 396, 394, 391,
    397, 376, 378, 377, 379, 391, 397, 392, 396, 393, 395, 394, 400, 378, 379, 400,
)


def gelu(p):
    t = jnp.minimum(p * p, GELU_CAP)
    q = jnp.full_like(t, GELU_P[-1])
    for coefficient in GELU_P[-2::-1]:
        q = q * t + coefficient
    half = 0.5 * p
    return half + half * jnp.tanh(p * q)


def tidy_block(total):
    n = total.shape[0]
    count = 256.0 * total[:, 128:129, :] + total[:, 129:130, :]
    return jnp.concatenate([total[:, :128, :], count_rows(count, n)], axis=1).astype(BF)


def count_rows(count, n):
    high = jnp.floor(count * (1.0 / 256.0))
    low = count - 256.0 * high
    row = lax.broadcasted_iota(jnp.int32, (n, 16, 128), 1)
    return jnp.where(row == 0, high, jnp.where(row == 1, low, 0.0))


def layer_kernel(
    tokens, w_up, w_down, stored, lengths_in, up_bias_in, down_bias_in, ln_gain_in, ln_bias_in, codes_in,
    e_out, f_out, lengths, up_bias, down_bias, ln_gain, ln_bias, codes,
    x_buf, gu, gd, acc, ps, pr, sv, tt, ra, rb, rc, ff, bb, em, er, ee, pooled,
    send_sem, recv_sem, local_sem,
):
    dp, s = lax.axis_index("dp"), lax.axis_index("sub")
    z, x, core = dp // NX, dp % NX, s % 2
    quarter = ((s // 2) % 2) * 2 + core

    def z_peer(k):
        return (((z + k + NZ) % NZ) * NX + x, s)

    def x_peer(k):
        return (z * NX + (x + k + NX) % NX, s)

    def s_peer(k):
        return (dp, (s + k) % NS)

    mate = (dp, s + 1 - 2 * core)
    partner = (dp, (s + 2 * core - 1 + NS) % NS)

    used = [0]
    sent = {}

    def remote(src, dst, device, arrival):
        return pltpu.make_async_remote_copy(
            src_ref=src, dst_ref=dst, send_sem=send_sem, recv_sem=arrival,
            device_id=device, device_id_type=MESH,
        )

    def local(src, dst):
        i = used[0]
        used[0] += 1
        copy = pltpu.make_async_copy(src, dst, local_sem.at[i])
        copy.start()
        return copy

    barrier = pltpu.get_barrier_semaphore()
    peers = [z_peer(k) for k in range(1, NZ)] + [x_peer(k) for k in range(1, NX)] + [s_peer(k) for k in range(1, NS)]
    for device in peers:
        pl.semaphore_signal(barrier, inc=1, device_id=device, device_id_type=MESH)

    row0 = pl.multiple_of(quarter * 32, 32)
    load_up = local(w_up.at[pl.ds(row0, 32)], gu.at[0, 0, 0])
    load_down = local(w_down.at[pl.ds(row0, 32)], gd.at[0, 0, 0])
    load_x = local(tokens, x_buf.at[0])
    load_bias = local(up_bias_in, up_bias)
    load_codes = local(codes_in, codes)
    load_s = local(stored, sv.at[:, pl.ds(0, 128)])
    load_rest = [local(lengths_in, lengths), local(down_bias_in, down_bias), local(ln_gain_in, ln_gain), local(ln_bias_in, ln_bias)]
    load_bias.wait()
    lane = lax.broadcasted_iota(jnp.int32, (8, 128), 1)
    own_bias = jnp.where(lane // 32 == quarter, jnp.broadcast_to(up_bias[...].astype(F32), (8, 128)), 0.0)
    own_bias = own_bias + pltpu.roll(own_bias, 64, 1)
    bb[0, 0] = own_bias + pltpu.roll(own_bias, 32, 1)
    sv[:, 128:256] = jnp.ones((2048, 128), BF)

    load_up.wait()
    load_down.wait()
    load_x.wait()
    pl.semaphore_wait(barrier, len(peers))

    copies = {}

    def piece(buffer, jx, slot, half=None):
        ref = buffer.at[slot // 4, jx, slot % 4]
        return ref if half is None else ref.at[pl.ds(16 * half, 16)]

    ways = ((1, SLOT_UP, 0), (-1, SLOT_DOWN, 1))
    for way, slots, half in ways:
        for k in range(1, 5):
            part = half if k == 4 else None
            copies[100 + 10 * half + k] = [
                (piece(gu, 0, slots[k - 1], part), piece(gu, 0, slots[k], part), z_peer(way))
            ]
            for jx in range(4):
                copies[200 + 20 * jx + 10 * half + k] = [
                    (piece(gd, jx, slots[k - 1], part), piece(gd, jx, slots[k], part), z_peer(way))
                ]
        near = 1 if way > 0 else 2
        for dz in range(-3, 5):
            slot = SLOT_UP[-dz] if dz < 0 else SLOT_DOWN[dz]
            copies[303 + 10 * half + dz] = [(piece(gu, 0, slot), piece(gu, near, slot), x_peer(way))]
            copies[323 + 10 * half + dz] = [(piece(gu, near, slot, half), piece(gu, 3, slot, half), x_peer(way))]
        copies[340 + half] = [(piece(gd, 0, 0), piece(gd, near, 0), x_peer(way))]
        copies[342 + half] = [(piece(gd, near, 0, half), piece(gd, 3, 0, half), x_peer(way))]

    def part_of(ref, j, size):
        return ref.at[pl.ds(size * j, size)]

    copies[350] = [(x_buf.at[0], x_buf.at[1], mate)]
    for j in range(4):
        copies[352 + j] = [(part_of(x_buf.at[0], j, 128), part_of(x_buf.at[2], j, 128), partner)]
        copies[356 + j] = [(part_of(x_buf.at[2], j, 128), part_of(x_buf.at[3], j, 128), mate)]
        copies[360 + j] = [(part_of(ps.at[1], j, 128), part_of(pr.at[2], j, 128), partner)]
    for i in range(2):
        copies[364 + i] = [(part_of(ps.at[0], i, 256), part_of(pr.at[0], i, 256), mate)]
        copies[366 + i] = [(part_of(ps.at[2], i, 256), part_of(pr.at[1], i, 256), mate)]
    copies[370] = [
        (bb.at[0, 0], bb.at[0, SLOT_UP[k] if k <= 4 else SLOT_DOWN[NZ - k]], z_peer(k)) for k in range(1, NZ)
    ]
    copies[371] = [(bb.at[0], bb.at[slot], x_peer(k)) for k, slot in ((1, 1), (-1, 2), (2, 3))]

    def x_blocks(k):
        return pl.multiple_of(((x + k + NX) % NX) * NZ, NZ)

    far, own = x_blocks(2), x_blocks(0)
    for way, slots, half in ways:
        copies[372 + half] = [(tt.at[pl.ds(far + 4 * half, 4)], ra.at[half], x_peer(way))]
        copies[374 + half] = [(tt.at[pl.ds(x_blocks(way), 8)], rb.at[half], x_peer(way))]
        copies[376 + half] = [(ff.at[pl.ds(own, 8)], ff.at[pl.ds(own, 8)], x_peer(way))]
        passed = ff.at[pl.ds(x_blocks(-way) + 4 * half, 4)]
        copies[378 + half] = [(passed, passed, x_peer(way))]
    copies[380] = [(tt.at[own + (z + k) % NZ], rc.at[k - 1], z_peer(k)) for k in range(1, NZ)]
    copies[381] = [(ff.at[own + z], ff.at[own + z], z_peer(k)) for k in range(1, NZ)]
    copies[382] = [(em.at[(s + k) % NS], er.at[s], s_peer(k)) for k in range(1, NS)]
    for k in range(NZ):
        if k:
            copies[390 + k] = [(ee.at[x, z], ee.at[x, z], z_peer(k))]
    copies[400] = [(ee.at[x], ee.at[x], x_peer(j)) for j in (2, 1, 3)]

    compute = {}

    def tally(first, last):
        def body(i, carry):
            delta = codes[...] - i * 256
            total = jnp.zeros((256, 256), F32)
            for part in range(4):
                row = lax.broadcasted_iota(jnp.int32, (256, 512), 0)
                hot = jnp.where(row == delta[:, 512 * part : 512 * (part + 1)], 1.0, 0.0).astype(BF)
                total = total + jnp.dot(hot, sv[512 * part : 512 * (part + 1), :], preferred_element_type=F32)
            for j in range(2):
                here = total[128 * j : 128 * (j + 1)]
                diagonal = lax.broadcasted_iota(jnp.int32, (128, 128), 0) == lax.broadcasted_iota(
                    jnp.int32, (128, 128), 1
                )
                count = jnp.sum(jnp.where(diagonal, here[:, 128:], 0.0), axis=0, keepdims=True)
                tt[2 * i + j, 0:128, :] = here[:, :128].astype(BF)
                tt[2 * i + j, 128:144, :] = count_rows(count[None], 1)[0].astype(BF)
            return carry

        lax.fori_loop(first, last, body, 0)

    for i in range(8):
        compute[i] = functools.partial(tally, 2 * i, 2 * i + 2)

    def add_into(base, count, others):
        def body(i, carry):
            total = tt[pl.ds(base + i, 1)].astype(F32)
            for ref in others:
                total = total + ref[pl.ds(i, 1)].astype(F32)
            tt[pl.ds(base + i, 1)] = tidy_block(total)
            return carry

        lax.fori_loop(0, count, body, 0)

    compute[8] = lambda: add_into(x_blocks(1), 4, [ra.at[0]])
    compute[9] = lambda: add_into(x_blocks(-1) + 4, 4, [ra.at[1]])
    compute[10] = lambda: add_into(own, 8, [rb.at[0], rb.at[1]])

    def add_z():
        total = tt[pl.ds(own + z, 1)].astype(F32)
        for k in range(1, NZ):
            total = total + rc[k - 1 : k].astype(F32)
        ff[pl.ds(own + z, 1)] = tidy_block(total)

    compute[11] = add_z

    def bias_of(h, first):
        lanes = lax.broadcasted_iota(jnp.int32, (1, 128), 1) // 32
        parts = []
        for jx in (first, first + 1):
            part = jnp.zeros((1, 128), F32)
            for i in range(4):
                part = jnp.where(lanes == i, bb[jx, 4 * h + i, 0:1, :], part)
            parts.append(part)
        return jnp.concatenate(parts, axis=1)

    def forward_tile(g, b, i, finish=None):
        h, first = g // 2, 2 * (g % 2)
        rows = pl.ds(256 * i, 256)
        up = gu[h, first : first + 2].reshape(256, 1024)
        down = gd[h, first : first + 2].reshape(256, 1024)
        pre = lax.dot_general(x_buf[b, rows, :], up, (((1,), (1,)), ((), ())), preferred_element_type=F32)
        hidden = gelu(pre + bias_of(h, first)).astype(BF)
        out = jnp.dot(hidden, down, preferred_element_type=F32)
        if g > 0:
            out = out + acc[b, rows, :]
        if finish is None:
            acc[b, rows, :] = out
        else:
            ps[finish, rows, :] = out.astype(BF)

    def forward(g, b):
        for i in range(2):
            forward_tile(g, b, i)

    for b in range(4):
        for g in range(3):
            compute[20 + 4 * g + b] = functools.partial(forward, g, b)
        for i in range(2):
            compute[40 + 2 * b + i] = functools.partial(forward_tile, 3, b, i, {3: 0, 1: 2}.get(b))

    def add_mate(j):
        rows = pl.ds(128 * j, 128)
        ps[1, rows, :] = (acc[2, rows, :] + pr[0, rows, :].astype(F32)).astype(BF)

    def place_of_passages():
        ends = [lengths[0, 0, 0]]
        for p in range(1, 4):
            ends.append(ends[-1] + lengths[0, 0, p])
        row8 = lax.broadcasted_iota(jnp.int32, (8, 1), 0)
        opening = jnp.full((8, 1), 0, jnp.int32)
        ending = jnp.full((8, 1), 0, jnp.int32)
        size = jnp.full((8, 1), 1, jnp.int32)
        for p in range(4):
            opening = jnp.where(row8 == p, ends[p] - lengths[0, 0, p], opening)
            ending = jnp.where(row8 == p, ends[p], ending)
            size = jnp.where(row8 == p, lengths[0, 0, p], size)
        return opening, ending, size

    def norm_rows(j):
        if j == 0:
            pooled[...] = jnp.zeros((8, 1024), F32)
        opening, ending, _ = place_of_passages()
        rows = pl.ds(128 * j, 128)
        resid = (
            x_buf[0, rows, :].astype(F32)
            + (acc[0, rows, :] + pr[1, rows, :].astype(F32) + pr[2, rows, :].astype(F32))
            + down_bias[...]
        )
        center = resid - jnp.mean(resid, axis=-1, keepdims=True)
        spread = jnp.mean(center * center, axis=-1, keepdims=True)
        layer_out = (center * lax.rsqrt(spread + 1e-12) * ln_gain[...] + ln_bias[...]).astype(BF)
        place = lax.broadcasted_iota(jnp.int32, (8, 128), 1) + 128 * j
        member = jnp.where((place >= opening) & (place < ending), 1.0, 0.0).astype(BF)
        pooled[...] += jnp.dot(member, layer_out, preferred_element_type=F32)

    for j in range(4):
        compute[50 + j] = functools.partial(add_mate, j)
        compute[54 + j] = functools.partial(norm_rows, j)

    def embed():
        _, _, size = place_of_passages()
        mean = pooled[...] / size.astype(F32)
        scaling = lax.rsqrt(jnp.mean(mean * mean, axis=-1, keepdims=True) + 1e-06)
        embedded = (mean * scaling).astype(BF).astype(F32)
        for i in range(NS):
            em[i] = embedded[:, 128 * i : 128 * (i + 1)]
        er[pl.ds(s, 1)] = em[pl.ds(s, 1)]

    def own_rows():
        low = lax.broadcasted_iota(jnp.int32, (8, 128), 0) < 4
        tiles = [jnp.where(low, er[2 * i], pltpu.roll(er[2 * i + 1], 4, 0)) for i in range(4)]
        ee[x, z] = jnp.concatenate(tiles, axis=0).astype(BF)

    compute[58] = embed
    compute[59] = own_rows

    landing = {
        370: bb.at[0, pl.ds(1, 7)], 371: bb.at[pl.ds(1, 3)], 380: rc, 381: rc, 382: er.at[pl.ds(1, 7)],
    }
    load_codes.wait()
    load_s.wait()
    for copy in load_rest:
        copy.wait()
    running = {}
    for name in ORDER:
        if name in running:
            running[name].wait_recv()
        elif name in copies:
            arrival = recv_sem.at[len(running)]
            for source, target, device in copies[name]:
                copy = remote(source, target, device, arrival)
                copy.start()
            if len(copies[name]) > 1:
                whole = landing.get(name)
                if whole is None:
                    whole = ee.at[pl.ds(0, 3)]
                copy = remote(whole, whole, device, arrival)
            running[name] = copy
        else:
            compute[name]()
    saves = [local(ff, f_out)] + [local(ee.at[i], e_out.at[:, i]) for i in range(NX)]
    total = 0
    for ends in copies.values():
        for source, _, _ in ends:
            total += source.size * source.dtype.itemsize
    for whole in (acc, x_buf, sv):
        size = whole.size * whole.dtype.itemsize
        for _ in range(total // size):
            pltpu.make_async_copy(whole, whole, send_sem).wait()
        total %= size
    rows = pl.ds(0, total // 32768 * 16)
    pltpu.make_async_copy(ps.at[0, rows], ps.at[0, rows], send_sem).wait()
    if total % 32768:
        tiles = pl.ds(0, total % 32768 // 4096)
        pltpu.make_async_copy(er.at[tiles], er.at[tiles], send_sem).wait()
    for copy in saves:
        copy.wait()


def update_kernel(
    e_in, codes_in, table_in, centroids_in, embeds, updated,
    e_all, new_codes, table, centroids, result, right, load_sem, save_sem,
):
    def load(i, source, target):
        copy = pltpu.make_async_copy(source, target, load_sem.at[i])
        copy.start()
        return copy

    first = [load(0, codes_in, new_codes), load(1, e_in, e_all)]
    parts = []
    for i in range(8):
        blocks, rows = pl.ds(4 * i, 4), pl.ds(512 * i, 512)
        parts.append(
            [
                load(2 + 2 * i, table_in.at[blocks], table.at[blocks]),
                load(3 + 2 * i, centroids_in.at[0, rows], centroids.at[rows]),
            ]
        )
    right[0:1024, 128:256] = jnp.ones((1024, 128), BF)
    lanes = lax.broadcasted_iota(jnp.int32, (128, 256), 1)
    right[1024:1152, :] = jnp.where(lanes >= 128, 256.0, 0.0).astype(BF)
    right[1152:1280, :] = jnp.where(lanes >= 128, 1.0, 0.0).astype(BF)
    diagonal = lax.broadcasted_iota(jnp.int32, (128, 128), 0) == lax.broadcasted_iota(
        jnp.int32, (128, 128), 1
    )
    row = lax.broadcasted_iota(jnp.int32, (128, 1024), 0)
    for copy in first:
        copy.wait()
    right[0:1024, 0:128] = e_all[...]
    mine = pl.multiple_of(lax.axis_index("dp") * 32, 32)
    save_own = pltpu.make_async_copy(e_all.at[pl.ds(mine, 32)], embeds, load_sem.at[0])
    save_own.start()
    saves = []
    for i in range(8):
        for copy in parts[i]:
            copy.wait()
        for j in range(4 * i, 4 * i + 4):
            rows = pl.ds(128 * j, 128)
            hot = jnp.where(row == new_codes[...] - 128 * j, 1.0, 0.0).astype(BF)
            high = jnp.where(diagonal, table[j, 128:129, :].astype(F32), 0.0).astype(BF)
            low = jnp.where(diagonal, table[j, 129:130, :].astype(F32), 0.0).astype(BF)
            left = jnp.concatenate([hot, high, low], axis=1)
            new = jnp.dot(left, right[...], preferred_element_type=F32)
            total = table[j, 0:128, :].astype(F32) + new[:, :128] + centroids[rows, :]
            result[rows, :] = total / (new[:, 128:] + 1.0)
        rows = pl.ds(512 * i, 512)
        copy = pltpu.make_async_copy(result.at[rows], updated.at[0, rows], save_sem.at[i])
        copy.start()
        saves.append(copy)
    save_own.wait()
    for copy in saves:
        copy.wait()


def on_device(
    tokens, lengths, w_up, up_bias, w_down, down_bias, ln_gain, ln_bias, stored, stored_codes, new_codes, centroids
):
    hbm = pl.BlockSpec(memory_space=pltpu.HBM)
    e_all, table = pl.pallas_call(
        layer_kernel,
        out_shape=(
            jax.ShapeDtypeStruct((NZ, NX, 32, 128), BF),
            jax.ShapeDtypeStruct((32, 144, 128), BF),
        ),
        in_specs=[hbm, hbm, hbm, hbm, hbm, hbm, hbm, hbm, hbm, hbm],
        out_specs=(hbm, hbm),
        scratch_shapes=[
            pltpu.SMEM((1, 1, 4), jnp.int32),
            pltpu.VMEM((1, 128), BF),
            pltpu.VMEM((1, 1024), F32),
            pltpu.VMEM((1, 1024), F32),
            pltpu.VMEM((1, 1024), F32),
            pltpu.VMEM((1, 2048), jnp.int32),
            pltpu.VMEM((4, 512, 1024), BF),
            pltpu.VMEM((2, 4, 4, 32, 1024), BF),
            pltpu.VMEM((2, 4, 4, 32, 1024), BF),
            pltpu.VMEM((4, 512, 1024), F32),
            pltpu.VMEM((3, 512, 1024), BF),
            pltpu.VMEM((3, 512, 1024), BF),
            pltpu.VMEM((2048, 256), BF),
            pltpu.VMEM((32, 144, 128), BF),
            pltpu.VMEM((2, 4, 144, 128), BF),
            pltpu.VMEM((2, 8, 144, 128), BF),
            pltpu.VMEM((7, 144, 128), BF),
            pltpu.VMEM((32, 144, 128), BF),
            pltpu.VMEM((4, 8, 8, 128), F32),
            pltpu.VMEM((8, 8, 128), F32),
            pltpu.VMEM((8, 8, 128), F32),
            pltpu.VMEM((NX, NZ, 32, 128), BF),
            pltpu.VMEM((8, 1024), F32),
            pltpu.SemaphoreType.DMA,
            pltpu.SemaphoreType.DMA((121,)),
            pltpu.SemaphoreType.DMA((16,)),
        ],
        compiler_params=pltpu.CompilerParams(
            collective_id=0, has_side_effects=True, vmem_limit_bytes=64 * 1024 * 1024
        ),
    )(
        tokens, w_up, w_down, stored, lengths, up_bias.reshape(1, 128), down_bias.reshape(1, 1024),
        ln_gain.reshape(1, 1024), ln_bias.reshape(1, 1024), stored_codes,
    )
    embeds, updated = pl.pallas_call(
        update_kernel,
        out_shape=(
            jax.ShapeDtypeStruct((32, 128), BF),
            jax.ShapeDtypeStruct((1, 4096, 128), F32),
        ),
        in_specs=[hbm, hbm, hbm, hbm],
        out_specs=(hbm, hbm),
        scratch_shapes=[
            pltpu.VMEM((1024, 128), BF),
            pltpu.VMEM((1, 1024), jnp.int32),
            pltpu.VMEM((32, 144, 128), BF),
            pltpu.VMEM((4096, 128), F32),
            pltpu.VMEM((4096, 128), F32),
            pltpu.VMEM((1280, 256), BF),
            pltpu.SemaphoreType.DMA((18,)),
            pltpu.SemaphoreType.DMA((8,)),
        ],
        compiler_params=pltpu.CompilerParams(vmem_limit_bytes=64 * 1024 * 1024),
    )(e_all.reshape(1024, 128), new_codes, table, centroids)
    return embeds, updated


def solution(mesh):
    return jax.shard_map(
        on_device,
        mesh=mesh,
        in_specs=(
            P(("dp", "sub"), None),
            P("dp", "sub", None),
            P("dp", None),
            P("dp"),
            P("dp", None),
            P(),
            P(),
            P(),
            P("dp", "sub"),
            P("sub", "dp"),
            P("sub", None),
            P("sub", None, None),
        ),
        out_specs=(P("dp", "sub"), P("sub", None, None)),
        check_vma=False,
    )
```

```python
import functools

import jax
import jax.numpy as jnp
from jax import lax
from jax.experimental import pallas as pl
from jax.experimental.pallas import tpu as pltpu
from jax.sharding import PartitionSpec as P

MESH = pl.DeviceIdType.MESH
NX, NZ, NS = 4, 8, 8
BF, F32 = jnp.bfloat16, jnp.float32

GELU_P = (
    0.7978849411010742,
    0.03633308410644531,
    -3.259497316321358e-05,
    -5.530619455385022e-05,
    3.964744792028796e-06,
    -1.322633664813111e-07,
    1.7561715415226331e-09,
)
GELU_CAP = 30.0

SLOT_UP = (0, 1, 3, 5, 7)
SLOT_DOWN = (0, 2, 4, 6, 7)


ORDER = (
    350, 340, 354, 111, 370, 353, 303, 341, 201, 0, 313, 1, 101, 211, 2, 3, 4, 352, 341, 241, 111, 340, 370, 251,
    350, 343, 342, 5, 304, 371, 221, 6, 313, 112, 211, 101, 303, 312, 7, 355, 323, 372, 373, 102, 314, 201, 231,
    202, 221, 222, 343, 212, 231, 241, 352, 232, 353, 302, 242, 251, 357, 342, 112, 212, 113, 315, 102, 261, 311,
    301, 222, 314, 355, 334, 323, 304, 354, 271, 305, 103, 333, 302, 252, 322, 202, 232, 373, 203, 324, 372, 8, 213,
    358, 261, 9, 375, 223, 301, 374, 356, 371, 262, 20, 233, 312, 321, 103, 271, 310, 311, 113, 242, 331, 358, 272,
    356, 252, 306, 324, 357, 322, 243, 333, 359, 332, 359, 253, 104, 305, 22, 262, 223, 114, 263, 203, 21, 213, 272,
    233, 273, 332, 23, 331, 321, 224, 315, 234, 300, 214, 243, 104, 114, 253, 334, 316, 204, 244, 254, 310, 263,
    317, 26, 325, 307, 27, 375, 264, 273, 274, 374, 10, 335, 380, 25, 234, 300, 306, 204, 330, 326, 316, 307, 320,
    336, 327, 317, 214, 337, 224, 31, 24, 264, 330, 274, 30, 29, 325, 326, 320, 336, 327, 244, 254, 337, 335, 46,
    364, 44, 47, 364, 50, 360, 380, 365, 11, 381, 42, 28, 365, 45, 52, 51, 362, 40, 366, 53, 43, 361, 366, 367, 367,
    363, 41, 381, 376, 377, 360, 362, 54, 361, 55, 56, 363, 57, 58, 382, 382, 59, 397, 392, 393, 395, 391, 394, 376,
    377, 378, 379, 396, 392, 394, 391, 396, 393, 397, 395, 400, 379, 378, 60, 400,
)


def gelu(p):
    t = jnp.minimum(p * p, GELU_CAP)
    q = jnp.full_like(t, GELU_P[-1])
    for coefficient in GELU_P[-2::-1]:
        q = q * t + coefficient
    half = 0.5 * p
    return half + half * jnp.tanh(p * q)


def tidy_block(total):
    n = total.shape[0]
    count = 256.0 * total[:, 128:129, :] + total[:, 129:130, :]
    return jnp.concatenate([total[:, :128, :], count_rows(count, n)], axis=1).astype(BF)


def count_rows(count, n):
    high = jnp.floor(count * (1.0 / 256.0))
    low = count - 256.0 * high
    row = lax.broadcasted_iota(jnp.int32, (n, 16, 128), 1)
    return jnp.where(row == 0, high, jnp.where(row == 1, low, 0.0))


def layer_kernel(
    tokens, w_up, w_down, stored, lengths_in, up_bias_in, down_bias_in, ln_gain_in, ln_bias_in, codes_in,
    e_out, f_out, lengths, up_bias, down_bias, ln_gain, ln_bias, codes,
    x_buf, gu, gd, acc, ps, pr, sv, tt, ra, rb, rc, ff, bb, em, er, ee, pooled,
    send_sem, recv_sem, local_sem,
):
    dp, s = lax.axis_index("dp"), lax.axis_index("sub")
    z, x, core = dp // NX, dp % NX, s % 2
    quarter = ((s // 2) % 2) * 2 + core

    def z_peer(k):
        return (((z + k + NZ) % NZ) * NX + x, s)

    def x_peer(k):
        return (z * NX + (x + k + NX) % NX, s)

    def s_peer(k):
        return (dp, (s + k) % NS)

    mate = (dp, s + 1 - 2 * core)
    partner = (dp, (s + 2 * core - 1 + NS) % NS)

    used = [0]
    sent = {}

    def remote(src, dst, device, arrival):
        return pltpu.make_async_remote_copy(
            src_ref=src, dst_ref=dst, send_sem=send_sem, recv_sem=arrival,
            device_id=device, device_id_type=MESH,
        )

    def local(src, dst):
        i = used[0]
        used[0] += 1
        copy = pltpu.make_async_copy(src, dst, local_sem.at[i])
        copy.start()
        return copy

    barrier = pltpu.get_barrier_semaphore()
    peers = [z_peer(k) for k in range(1, NZ)] + [x_peer(k) for k in range(1, NX)] + [s_peer(k) for k in range(1, NS)]
    for device in peers:
        pl.semaphore_signal(barrier, inc=1, device_id=device, device_id_type=MESH)

    row0 = pl.multiple_of(quarter * 32, 32)
    load_up = local(w_up.at[pl.ds(row0, 32)], gu.at[0, 0, 0])
    load_down = local(w_down.at[pl.ds(row0, 32)], gd.at[0, 0, 0])
    load_x = local(tokens, x_buf.at[0])
    load_bias = local(up_bias_in, up_bias)
    load_codes = local(codes_in, codes)
    load_s = local(stored, sv.at[:, pl.ds(0, 128)])
    load_rest = [local(lengths_in, lengths), local(down_bias_in, down_bias), local(ln_gain_in, ln_gain), local(ln_bias_in, ln_bias)]
    load_bias.wait()
    lane = lax.broadcasted_iota(jnp.int32, (8, 128), 1)
    own_bias = jnp.where(lane // 32 == quarter, jnp.broadcast_to(up_bias[...].astype(F32), (8, 128)), 0.0)
    own_bias = own_bias + pltpu.roll(own_bias, 64, 1)
    bb[0, 0] = own_bias + pltpu.roll(own_bias, 32, 1)
    sv[:, 128:256] = jnp.ones((2048, 128), BF)

    load_up.wait()
    load_down.wait()
    load_x.wait()
    pl.semaphore_wait(barrier, len(peers))

    copies = {}

    def piece(buffer, jx, slot, half=None):
        ref = buffer.at[slot // 4, jx, slot % 4]
        return ref if half is None else ref.at[pl.ds(16 * half, 16)]

    ways = ((1, SLOT_UP, 0), (-1, SLOT_DOWN, 1))
    for way, slots, half in ways:
        for k in range(1, 5):
            part = half if k == 4 else None
            copies[100 + 10 * half + k] = [
                (piece(gu, 0, slots[k - 1], part), piece(gu, 0, slots[k], part), z_peer(way))
            ]
            for jx in range(4):
                copies[200 + 20 * jx + 10 * half + k] = [
                    (piece(gd, jx, slots[k - 1], part), piece(gd, jx, slots[k], part), z_peer(way))
                ]
        near = 1 if way > 0 else 2
        for dz in range(-3, 5):
            slot = SLOT_UP[-dz] if dz < 0 else SLOT_DOWN[dz]
            copies[303 + 10 * half + dz] = [(piece(gu, 0, slot), piece(gu, near, slot), x_peer(way))]
            copies[323 + 10 * half + dz] = [(piece(gu, near, slot, half), piece(gu, 3, slot, half), x_peer(way))]
        copies[340 + half] = [(piece(gd, 0, 0), piece(gd, near, 0), x_peer(way))]
        copies[342 + half] = [(piece(gd, near, 0, half), piece(gd, 3, 0, half), x_peer(way))]

    def part_of(ref, j, size):
        return ref.at[pl.ds(size * j, size)]

    copies[350] = [(x_buf.at[0], x_buf.at[1], mate)]
    for j in range(4):
        copies[352 + j] = [(part_of(x_buf.at[0], j, 128), part_of(x_buf.at[2], j, 128), partner)]
        copies[356 + j] = [(part_of(x_buf.at[2], j, 128), part_of(x_buf.at[3], j, 128), mate)]
        copies[360 + j] = [(part_of(ps.at[1], j, 128), part_of(pr.at[2], j, 128), partner)]
    for i in range(2):
        copies[364 + i] = [(part_of(ps.at[0], i, 256), part_of(pr.at[0], i, 256), mate)]
        copies[366 + i] = [(part_of(ps.at[2], i, 256), part_of(pr.at[1], i, 256), mate)]
    copies[370] = [
        (bb.at[0, 0], bb.at[0, SLOT_UP[k] if k <= 4 else SLOT_DOWN[NZ - k]], z_peer(k)) for k in range(1, NZ)
    ]
    copies[371] = [(bb.at[0], bb.at[slot], x_peer(k)) for k, slot in ((1, 1), (-1, 2), (2, 3))]

    def x_blocks(k):
        return pl.multiple_of(((x + k + NX) % NX) * NZ, NZ)

    far, own = x_blocks(2), x_blocks(0)
    for way, slots, half in ways:
        copies[372 + half] = [(tt.at[pl.ds(far + 4 * half, 4)], ra.at[half], x_peer(way))]
        copies[374 + half] = [(tt.at[pl.ds(x_blocks(way), 8)], rb.at[half], x_peer(way))]
        copies[376 + half] = [(ff.at[pl.ds(own, 8)], ff.at[pl.ds(own, 8)], x_peer(way))]
        passed = ff.at[pl.ds(x_blocks(-way) + 4 * half, 4)]
        copies[378 + half] = [(passed, passed, x_peer(way))]
    copies[380] = [(tt.at[own + (z + k) % NZ], rc.at[k - 1], z_peer(k)) for k in range(1, NZ)]
    copies[381] = [(ff.at[own + z], ff.at[own + z], z_peer(k)) for k in range(1, NZ)]
    copies[382] = [(em.at[(s + k) % NS], er.at[s], s_peer(k)) for k in range(1, NS)]
    for k in range(NZ):
        if k:
            copies[390 + k] = [(ee.at[x, z], ee.at[x, z], z_peer(k))]
    copies[400] = [(ee.at[x], ee.at[x], x_peer(j)) for j in (2, 1, 3)]

    compute = {}

    def tally(first, last):
        def body(i, carry):
            delta = codes[...] - i * 256
            total = jnp.zeros((256, 256), F32)
            for part in range(4):
                row = lax.broadcasted_iota(jnp.int32, (256, 512), 0)
                hot = jnp.where(row == delta[:, 512 * part : 512 * (part + 1)], 1.0, 0.0).astype(BF)
                total = total + jnp.dot(hot, sv[512 * part : 512 * (part + 1), :], preferred_element_type=F32)
            for j in range(2):
                here = total[128 * j : 128 * (j + 1)]
                diagonal = lax.broadcasted_iota(jnp.int32, (128, 128), 0) == lax.broadcasted_iota(
                    jnp.int32, (128, 128), 1
                )
                count = jnp.sum(jnp.where(diagonal, here[:, 128:], 0.0), axis=0, keepdims=True)
                tt[2 * i + j, 0:128, :] = here[:, :128].astype(BF)
                tt[2 * i + j, 128:144, :] = count_rows(count[None], 1)[0].astype(BF)
            return carry

        lax.fori_loop(first, last, body, 0)

    for i in range(8):
        compute[i] = functools.partial(tally, 2 * i, 2 * i + 2)

    def add_into(base, count, others):
        def body(i, carry):
            total = tt[pl.ds(base + i, 1)].astype(F32)
            for ref in others:
                total = total + ref[pl.ds(i, 1)].astype(F32)
            tt[pl.ds(base + i, 1)] = tidy_block(total)
            return carry

        lax.fori_loop(0, count, body, 0)

    compute[8] = lambda: add_into(x_blocks(1), 4, [ra.at[0]])
    compute[9] = lambda: add_into(x_blocks(-1) + 4, 4, [ra.at[1]])
    compute[10] = lambda: add_into(own, 8, [rb.at[0], rb.at[1]])

    def add_z():
        total = tt[pl.ds(own + z, 1)].astype(F32)
        for k in range(1, NZ):
            total = total + rc[k - 1 : k].astype(F32)
        ff[pl.ds(own + z, 1)] = tidy_block(total)

    compute[11] = add_z

    def bias_of(h, first):
        lanes = lax.broadcasted_iota(jnp.int32, (1, 128), 1) // 32
        parts = []
        for jx in (first, first + 1):
            part = jnp.zeros((1, 128), F32)
            for i in range(4):
                part = jnp.where(lanes == i, bb[jx, 4 * h + i, 0:1, :], part)
            parts.append(part)
        return jnp.concatenate(parts, axis=1)

    def forward_tile(g, b, i, finish=None):
        h, first = g // 2, 2 * (g % 2)
        rows = pl.ds(256 * i, 256)
        up = gu[h, first : first + 2].reshape(256, 1024)
        down = gd[h, first : first + 2].reshape(256, 1024)
        pre = lax.dot_general(x_buf[b, rows, :], up, (((1,), (1,)), ((), ())), preferred_element_type=F32)
        hidden = gelu(pre + bias_of(h, first)).astype(BF)
        out = jnp.dot(hidden, down, preferred_element_type=F32)
        if g > 0:
            out = out + acc[b, rows, :]
        if finish is None:
            acc[b, rows, :] = out
        else:
            ps[finish, rows, :] = out.astype(BF)

    def forward(g, b):
        for i in range(2):
            forward_tile(g, b, i)

    for b in range(4):
        for g in range(3):
            compute[20 + 4 * g + b] = functools.partial(forward, g, b)
        for i in range(2):
            compute[40 + 2 * b + i] = functools.partial(forward_tile, 3, b, i, {3: 0, 1: 2}.get(b))

    def add_mate(j):
        rows = pl.ds(128 * j, 128)
        ps[1, rows, :] = (acc[2, rows, :] + pr[0, rows, :].astype(F32)).astype(BF)

    def place_of_passages():
        ends = [lengths[0, 0, 0]]
        for p in range(1, 4):
            ends.append(ends[-1] + lengths[0, 0, p])
        row8 = lax.broadcasted_iota(jnp.int32, (8, 1), 0)
        opening = jnp.full((8, 1), 0, jnp.int32)
        ending = jnp.full((8, 1), 0, jnp.int32)
        size = jnp.full((8, 1), 1, jnp.int32)
        for p in range(4):
            opening = jnp.where(row8 == p, ends[p] - lengths[0, 0, p], opening)
            ending = jnp.where(row8 == p, ends[p], ending)
            size = jnp.where(row8 == p, lengths[0, 0, p], size)
        return opening, ending, size

    def norm_rows(j):
        if j == 0:
            pooled[...] = jnp.zeros((8, 1024), F32)
        opening, ending, _ = place_of_passages()
        rows = pl.ds(128 * j, 128)
        resid = (
            x_buf[0, rows, :].astype(F32)
            + (acc[0, rows, :] + pr[1, rows, :].astype(F32) + pr[2, rows, :].astype(F32))
            + down_bias[...]
        )
        center = resid - jnp.mean(resid, axis=-1, keepdims=True)
        spread = jnp.mean(center * center, axis=-1, keepdims=True)
        layer_out = (center * lax.rsqrt(spread + 1e-12) * ln_gain[...] + ln_bias[...]).astype(BF)
        place = lax.broadcasted_iota(jnp.int32, (8, 128), 1) + 128 * j
        member = jnp.where((place >= opening) & (place < ending), 1.0, 0.0).astype(BF)
        pooled[...] += jnp.dot(member, layer_out, preferred_element_type=F32)

    for j in range(4):
        compute[50 + j] = functools.partial(add_mate, j)
        compute[54 + j] = functools.partial(norm_rows, j)

    def embed():
        _, _, size = place_of_passages()
        mean = pooled[...] / size.astype(F32)
        scaling = lax.rsqrt(jnp.mean(mean * mean, axis=-1, keepdims=True) + 1e-06)
        embedded = (mean * scaling).astype(BF).astype(F32)
        for i in range(NS):
            em[i] = embedded[:, 128 * i : 128 * (i + 1)]
        er[pl.ds(s, 1)] = em[pl.ds(s, 1)]

    def own_rows():
        low = lax.broadcasted_iota(jnp.int32, (8, 128), 0) < 4
        tiles = [jnp.where(low, er[2 * i], pltpu.roll(er[2 * i + 1], 4, 0)) for i in range(4)]
        ee[x, z] = jnp.concatenate(tiles, axis=0).astype(BF)

    compute[58] = embed
    compute[59] = own_rows
    saves = []
    compute[60] = lambda: saves.append(local(ff, f_out))

    landing = {
        370: bb.at[0, pl.ds(1, 7)], 371: bb.at[pl.ds(1, 3)], 380: rc, 381: rc, 382: er.at[pl.ds(1, 7)],
    }
    load_codes.wait()
    load_s.wait()
    for copy in load_rest:
        copy.wait()
    running = {}
    for name in ORDER:
        if name in running:
            running[name].wait_recv()
        elif name in copies:
            arrival = recv_sem.at[len(running)]
            for source, target, device in copies[name]:
                copy = remote(source, target, device, arrival)
                copy.start()
            if len(copies[name]) > 1:
                whole = landing.get(name)
                if whole is None:
                    whole = ee.at[pl.ds(0, 3)]
                copy = remote(whole, whole, device, arrival)
            running[name] = copy
        else:
            compute[name]()
    saves += [local(ee.at[i], e_out.at[:, i]) for i in range(NX)]
    total = 0
    for ends in copies.values():
        for source, _, _ in ends:
            total += source.size * source.dtype.itemsize
    for whole in (acc, x_buf, sv):
        size = whole.size * whole.dtype.itemsize
        for _ in range(total // size):
            pltpu.make_async_copy(whole, whole, send_sem).wait()
        total %= size
    rows = pl.ds(0, total // 32768 * 16)
    pltpu.make_async_copy(ps.at[0, rows], ps.at[0, rows], send_sem).wait()
    if total % 32768:
        tiles = pl.ds(0, total % 32768 // 4096)
        pltpu.make_async_copy(er.at[tiles], er.at[tiles], send_sem).wait()
    for copy in saves:
        copy.wait()


def update_kernel(
    e_in, codes_in, table_in, centroids_in, embeds, updated,
    e_all, new_codes, table, centroids, result, right, load_sem, save_sem,
):
    def load(i, source, target):
        copy = pltpu.make_async_copy(source, target, load_sem.at[i])
        copy.start()
        return copy

    first = [load(0, codes_in, new_codes), load(1, e_in, e_all)]
    parts = []
    for i in range(8):
        blocks, rows = pl.ds(4 * i, 4), pl.ds(512 * i, 512)
        parts.append(
            [
                load(2 + 2 * i, table_in.at[blocks], table.at[blocks]),
                load(3 + 2 * i, centroids_in.at[0, rows], centroids.at[rows]),
            ]
        )
    right[0:1024, 128:256] = jnp.ones((1024, 128), BF)
    lanes = lax.broadcasted_iota(jnp.int32, (128, 256), 1)
    right[1024:1152, :] = jnp.where(lanes >= 128, 256.0, 0.0).astype(BF)
    right[1152:1280, :] = jnp.where(lanes >= 128, 1.0, 0.0).astype(BF)
    diagonal = lax.broadcasted_iota(jnp.int32, (128, 128), 0) == lax.broadcasted_iota(
        jnp.int32, (128, 128), 1
    )
    row = lax.broadcasted_iota(jnp.int32, (128, 1024), 0)
    for copy in first:
        copy.wait()
    right[0:1024, 0:128] = e_all[...]
    mine = pl.multiple_of(lax.axis_index("dp") * 32, 32)
    save_own = pltpu.make_async_copy(e_all.at[pl.ds(mine, 32)], embeds, load_sem.at[0])
    save_own.start()
    saves = []
    for i in range(8):
        for copy in parts[i]:
            copy.wait()
        for j in range(4 * i, 4 * i + 4):
            rows = pl.ds(128 * j, 128)
            hot = jnp.where(row == new_codes[...] - 128 * j, 1.0, 0.0).astype(BF)
            high = jnp.where(diagonal, table[j, 128:129, :].astype(F32), 0.0).astype(BF)
            low = jnp.where(diagonal, table[j, 129:130, :].astype(F32), 0.0).astype(BF)
            left = jnp.concatenate([hot, high, low], axis=1)
            new = jnp.dot(left, right[...], preferred_element_type=F32)
            total = table[j, 0:128, :].astype(F32) + new[:, :128] + centroids[rows, :]
            result[rows, :] = total / (new[:, 128:] + 1.0)
        rows = pl.ds(512 * i, 512)
        copy = pltpu.make_async_copy(result.at[rows], updated.at[0, rows], save_sem.at[i])
        copy.start()
        saves.append(copy)
    save_own.wait()
    for copy in saves:
        copy.wait()


def on_device(
    tokens, lengths, w_up, up_bias, w_down, down_bias, ln_gain, ln_bias, stored, stored_codes, new_codes, centroids
):
    hbm = pl.BlockSpec(memory_space=pltpu.HBM)
    e_all, table = pl.pallas_call(
        layer_kernel,
        out_shape=(
            jax.ShapeDtypeStruct((NZ, NX, 32, 128), BF),
            jax.ShapeDtypeStruct((32, 144, 128), BF),
        ),
        in_specs=[hbm, hbm, hbm, hbm, hbm, hbm, hbm, hbm, hbm, hbm],
        out_specs=(hbm, hbm),
        scratch_shapes=[
            pltpu.SMEM((1, 1, 4), jnp.int32),
            pltpu.VMEM((1, 128), BF),
            pltpu.VMEM((1, 1024), F32),
            pltpu.VMEM((1, 1024), F32),
            pltpu.VMEM((1, 1024), F32),
            pltpu.VMEM((1, 2048), jnp.int32),
            pltpu.VMEM((4, 512, 1024), BF),
            pltpu.VMEM((2, 4, 4, 32, 1024), BF),
            pltpu.VMEM((2, 4, 4, 32, 1024), BF),
            pltpu.VMEM((4, 512, 1024), F32),
            pltpu.VMEM((3, 512, 1024), BF),
            pltpu.VMEM((3, 512, 1024), BF),
            pltpu.VMEM((2048, 256), BF),
            pltpu.VMEM((32, 144, 128), BF),
            pltpu.VMEM((2, 4, 144, 128), BF),
            pltpu.VMEM((2, 8, 144, 128), BF),
            pltpu.VMEM((7, 144, 128), BF),
            pltpu.VMEM((32, 144, 128), BF),
            pltpu.VMEM((4, 8, 8, 128), F32),
            pltpu.VMEM((8, 8, 128), F32),
            pltpu.VMEM((8, 8, 128), F32),
            pltpu.VMEM((NX, NZ, 32, 128), BF),
            pltpu.VMEM((8, 1024), F32),
            pltpu.SemaphoreType.DMA,
            pltpu.SemaphoreType.DMA((121,)),
            pltpu.SemaphoreType.DMA((16,)),
        ],
        compiler_params=pltpu.CompilerParams(
            collective_id=0, has_side_effects=True, vmem_limit_bytes=64 * 1024 * 1024
        ),
    )(
        tokens, w_up, w_down, stored, lengths, up_bias.reshape(1, 128), down_bias.reshape(1, 1024),
        ln_gain.reshape(1, 1024), ln_bias.reshape(1, 1024), stored_codes,
    )
    embeds, updated = pl.pallas_call(
        update_kernel,
        out_shape=(
            jax.ShapeDtypeStruct((32, 128), BF),
            jax.ShapeDtypeStruct((1, 4096, 128), F32),
        ),
        in_specs=[hbm, hbm, hbm, hbm],
        out_specs=(hbm, hbm),
        scratch_shapes=[
            pltpu.VMEM((1024, 128), BF),
            pltpu.VMEM((1, 1024), jnp.int32),
            pltpu.VMEM((32, 144, 128), BF),
            pltpu.VMEM((4096, 128), F32),
            pltpu.VMEM((4096, 128), F32),
            pltpu.VMEM((1280, 256), BF),
            pltpu.SemaphoreType.DMA((18,)),
            pltpu.SemaphoreType.DMA((8,)),
        ],
        compiler_params=pltpu.CompilerParams(vmem_limit_bytes=64 * 1024 * 1024),
    )(e_all.reshape(1024, 128), new_codes, table, centroids)
    return embeds, updated


def solution(mesh):
    return jax.shard_map(
        on_device,
        mesh=mesh,
        in_specs=(
            P(("dp", "sub"), None),
            P("dp", "sub", None),
            P("dp", None),
            P("dp"),
            P("dp", None),
            P(),
            P(),
            P(),
            P("dp", "sub"),
            P("sub", "dp"),
            P("sub", None),
            P("sub", None, None),
        ),
        out_specs=(P("dp", "sub"), P("sub", None, None)),
        check_vma=False,
    )
```
